512 devices in a mesh: frame: 16 (over y_lo, x, core), row: 8 (over z), head: 4 (over y_hi).
Axes of the slice: x: 4, y: 8 (y_hi: 4, y_lo: 2; y = y_hi * 2 + y_lo), z: 8, core: 2. Of those that a mesh axis runs over, the one named last changes fastest.
Arguments:
- queries: bfloat16 [96, 32, 8, 1536], P('frame', 'row', None, 'head'), may hold values from -6 to 6
- key_tokens: bfloat16 [96, 32, 8, 1536], P('frame', 'row', None, 'head'), may hold values from -6 to 6
- value_tokens: bfloat16 [96, 32, 8, 1536], P('frame', 'row', None, 'head'), may hold values from -6 to 6
- grad_out: bfloat16 [96, 32, 8, 1536], P('frame', 'row', None, 'head'), may hold values from -6 to 6
- tile_pairs: int32 [16, 8, 1, 27], P('frame', 'row'), may hold values from 0 to 1, as said below
Outputs:
- attended: bfloat16 [96, 32, 8, 1536], P('frame', 'row', 'head')
- query_grad: bfloat16 [96, 32, 8, 1536], P('frame', 'row', 'head')
- key_grad: bfloat16 [96, 32, 8, 1536], P('frame', 'row', 'head')
- value_grad: bfloat16 [96, 32, 8, 1536], P('frame', 'row', 'head')
The draws below stay inside these ranges and needn't reach their ends.
Inputs may be any that keep to these rules, and one draw needn't show every extreme that they name: tile_pairs[t, 13], the pair of a tile with itself, is 1 for every tile t.
All inputs are finite; a program needn't handle non-finite values.
Results may differ from the reference program's by a relative error of at most 0.012.
The reference program's roundings to bfloat16 on the way (of `rounded` and `slopes`) count: a program that leaves them out, or rounds other values in their place, can miss the bound.
Values may be sent and summed in bfloat16 or wider, within the bound.
No kernel may reach another device: no remote copies, remote signals or barrier semaphores. Data moves between devices by JAX's collectives and lax.ppermute only.
A program may use at most 64 MiB of HBM per device.

```python
import jax
import jax.numpy as jnp
from jax import lax

HEADS = 12
HEAD_DIM = 128
COLS = 8
TILE_F = 6
TILE_R = 4
TILE_C = 8
FRAMES = 96
ROWS = 32


def draw_queries(key, part):
    key = jax.random.fold_in(key, 11)
    grid_shape = (FRAMES, ROWS, COLS // TILE_C, TILE_C, HEADS * HEAD_DIM)
    sample = jnp.clip(jax.random.normal(key, grid_shape, jnp.float32), -6.0, 6.0)
    return sample.reshape(FRAMES, ROWS, COLS, HEADS * HEAD_DIM).astype(jnp.bfloat16)


def draw_key_tokens(key, part):
    key = jax.random.fold_in(key, 23)
    grid_shape = (FRAMES, ROWS, COLS // TILE_C, TILE_C, HEADS * HEAD_DIM)
    sample = jnp.clip(jax.random.normal(key, grid_shape, jnp.float32), -6.0, 6.0)
    return sample.reshape(FRAMES, ROWS, COLS, HEADS * HEAD_DIM).astype(jnp.bfloat16)


def draw_tile_pairs(key, part):
    key = jax.random.fold_in(key, 7)
    level_key, bit_key = jax.random.split(key)
    grid_shape = (FRAMES // TILE_F, ROWS // TILE_R, COLS // TILE_C)
    levels = jax.random.randint(level_key, grid_shape + (1,), 1, 5)
    pair_bits = (jax.random.randint(bit_key, grid_shape + (27,), 0, 4) < levels).astype(jnp.int32)
    center = (jnp.arange(27) == 13)[None, None, None, :]
    return jnp.where(center, 1, pair_bits).astype(jnp.int32)


def shard_levels(own_key, extent, shards, least, top_value):
    gain, own = 1.0, jax.random.fold_in(own_key, 6)
    for dim, parts in shards:
        steps = jnp.exp(jax.random.uniform(jax.random.fold_in(own, dim), (parts,), jnp.float32, least / len(shards), top_value / len(shards)))
        gain = gain * jnp.repeat(steps, extent[dim] // parts).reshape([-1 if axis == dim else 1 for axis in range(len(extent))])
    return gain


def scatter_about(stream_key, dims, width, limit, shards=(), kind=jnp.bfloat16):
    array = jax.random.normal(stream_key, dims, jnp.float32) * width
    if len(shards) > 0:
        array = shard_levels(stream_key, dims, shards, -0.22, 0.18) * array
    return jnp.clip(array, min=-limit, max=limit).astype(kind)


def setup_inputs(seed: int = 0) -> dict:
    streams_of = jax.random.split(jax.random.key(seed), 6)
    return {
        "queries": draw_queries(jax.random.fold_in(streams_of[5], 71), 0),
        "key_tokens": draw_key_tokens(jax.random.fold_in(streams_of[5], 71), 0),
        "value_tokens": scatter_about(streams_of[2], (FRAMES, ROWS, COLS, HEADS * HEAD_DIM), 1.0, 6.0, ((0, 16), (1, 8), (3, 4))),
        "grad_out": scatter_about(streams_of[3], (FRAMES, ROWS, COLS, HEADS * HEAD_DIM), 1.0, 6.0, ((0, 16), (1, 8), (3, 4))),
        "tile_pairs": draw_tile_pairs(jax.random.fold_in(streams_of[5], 71), 0),
    }


def offset_table(inner_count, outer_count, tile_len, direction_sign, offset_add):
    near_tiles = jnp.arange(inner_count, dtype=jnp.int32) // tile_len
    far_tiles = jnp.arange(outer_count, dtype=jnp.int32) // tile_len
    offsets = direction_sign * (far_tiles[None, :] - near_tiles[:, None]) + offset_add
    return (offsets[:, :, None] == jnp.arange(3, dtype=jnp.int32)[None, None, :]).astype(jnp.float32)


def tile_tokens(pattern, span_f, span_r, span_c):
    grown_grid = jnp.repeat(jnp.repeat(jnp.repeat(pattern, span_f, axis=0), span_r, axis=1), span_c, axis=2)
    return grown_grid.reshape(grown_grid.shape[:3] + (3, 3, 3)).astype(jnp.float32)


def reference(queries, key_tokens, value_tokens, grad_out, tile_pairs):
    scaling = HEAD_DIM ** -0.5
    tiles_f = FRAMES // TILE_F
    tiles_r = ROWS // TILE_R
    feat_width = HEADS * HEAD_DIM
    slab_size = TILE_F * TILE_R * COLS
    wide_size = 9 * slab_size
    margin = ((TILE_F, TILE_F), (TILE_R, TILE_R), (0, 0), (0, 0))
    key_pad = jnp.pad(key_tokens, margin)
    value_pad = jnp.pad(value_tokens, margin)
    column_table = offset_table(COLS, COLS, TILE_C, 1, 1)
    span_f = jnp.arange(3 * TILE_F, dtype=jnp.int32)
    span_r = jnp.arange(3 * TILE_R, dtype=jnp.int32)
    anchor = jnp.zeros((), jnp.int32)

    def split_heads(source, row_count):
        return source.reshape(row_count, HEADS, HEAD_DIM).astype(jnp.float32)

    def to_grid(blocks):
        shaped = blocks.reshape((tiles_f, tiles_r, TILE_F, TILE_R, COLS, blocks.shape[-1]))
        return shaped.transpose(0, 2, 1, 3, 4, 5).reshape(FRAMES, ROWS, COLS, blocks.shape[-1])

    def forward_slab(slab_index):
        tile_a = slab_index // tiles_r
        tile_b = slab_index % tiles_r
        start_f = (tile_a * TILE_F).astype(jnp.int32)
        start_r = (tile_b * TILE_R).astype(jnp.int32)
        corner = (start_f, start_r, anchor, anchor)
        query_now = split_heads(lax.dynamic_slice(queries, corner, (TILE_F, TILE_R, COLS, feat_width)), slab_size)
        grad_now = split_heads(lax.dynamic_slice(grad_out, corner, (TILE_F, TILE_R, COLS, feat_width)), slab_size)
        key_near = split_heads(lax.dynamic_slice(key_pad, corner, (3 * TILE_F, 3 * TILE_R, COLS, feat_width)), wide_size)
        value_near = split_heads(lax.dynamic_slice(value_pad, corner, (3 * TILE_F, 3 * TILE_R, COLS, feat_width)), wide_size)
        pattern = lax.dynamic_slice(tile_pairs, (tile_a.astype(jnp.int32), tile_b.astype(jnp.int32), anchor, anchor), (1, 1, COLS // TILE_C, 27))
        pattern_tok = tile_tokens(pattern, TILE_F, TILE_R, TILE_C)
        cells_f = start_f - TILE_F + span_f
        cells_r = start_r - TILE_R + span_r
        inside_f = ((cells_f >= 0) & (cells_f < FRAMES)).astype(jnp.float32)
        inside_r = ((cells_r >= 0) & (cells_r < ROWS)).astype(jnp.float32)
        table_f = offset_table(TILE_F, 3 * TILE_F, TILE_F, 1, 0) * inside_f[None, :, None]
        table_r = offset_table(TILE_R, 3 * TILE_R, TILE_R, 1, 0) * inside_r[None, :, None]
        allowed = jnp.einsum("frcxyz,fex,rgy,chz->frcegh", pattern_tok, table_f, table_r, column_table).reshape(slab_size, wide_size) > 0.5
        scores = jnp.einsum("qhd,khd->hqk", query_now, key_near) * scaling
        scores = jnp.where(allowed[None], scores, -jnp.inf)
        row_max = jnp.max(scores, axis=2)
        weights = jnp.exp(scores - row_max[:, :, None])
        row_sum = jnp.sum(weights, axis=2)
        weights = weights / row_sum[:, :, None]
        rounded = weights.astype(jnp.bfloat16)
        attended = jnp.einsum("hqk,khd->qhd", rounded.astype(jnp.float32), value_near).astype(jnp.bfloat16)
        spread = jnp.einsum("qhd,qhd->hq", grad_now, attended.astype(jnp.float32))
        pushes = jnp.einsum("qhd,khd->hqk", grad_now, value_near)
        slopes = (weights * (pushes - spread[:, :, None])).astype(jnp.bfloat16)
        query_grad = (scaling * jnp.einsum("hqk,khd->qhd", slopes.astype(jnp.float32), key_near)).astype(jnp.bfloat16)
        summary = jnp.stack([row_max, row_sum - 1.0, spread])
        return (attended.reshape(TILE_F, TILE_R, COLS, feat_width), query_grad.reshape(TILE_F, TILE_R, COLS, feat_width), summary)

    slab_ids = jnp.arange(tiles_f * tiles_r, dtype=jnp.int32)
    attended_blocks, query_blocks, summary_blocks = lax.map(forward_slab, slab_ids)
    attended = to_grid(attended_blocks)
    query_grad = to_grid(query_blocks)
    summary_tok = summary_blocks.reshape(tiles_f * tiles_r, 3 * HEADS, TILE_F, TILE_R, COLS).transpose(0, 2, 3, 4, 1)
    stat_grid = to_grid(summary_tok).reshape(FRAMES, ROWS, COLS, 3, HEADS)
    stat_pad = jnp.pad(stat_grid, ((TILE_F, TILE_F), (TILE_R, TILE_R), (0, 0), (0, 0), (0, 0)))
    query_pad = jnp.pad(queries, margin)
    grad_pad = jnp.pad(grad_out, margin)
    pattern_pad = jnp.pad(tile_pairs, ((1, 1), (1, 1), (0, 0), (0, 0)))
    key_table_f = offset_table(TILE_F, 3 * TILE_F, TILE_F, -1, 2)
    key_table_r = offset_table(TILE_R, 3 * TILE_R, TILE_R, -1, 2)
    key_column = offset_table(COLS, COLS, TILE_C, -1, 1)

    def backward_slab(slab_index):
        tile_a = slab_index // tiles_r
        tile_b = slab_index % tiles_r
        start_f = (tile_a * TILE_F).astype(jnp.int32)
        start_r = (tile_b * TILE_R).astype(jnp.int32)
        corner = (start_f, start_r, anchor, anchor)
        key_now = split_heads(lax.dynamic_slice(key_tokens, corner, (TILE_F, TILE_R, COLS, feat_width)), slab_size)
        value_now = split_heads(lax.dynamic_slice(value_tokens, corner, (TILE_F, TILE_R, COLS, feat_width)), slab_size)
        query_near = split_heads(lax.dynamic_slice(query_pad, corner, (3 * TILE_F, 3 * TILE_R, COLS, feat_width)), wide_size)
        grad_near = split_heads(lax.dynamic_slice(grad_pad, corner, (3 * TILE_F, 3 * TILE_R, COLS, feat_width)), wide_size)
        stat_near = lax.dynamic_slice(stat_pad, (start_f, start_r, anchor, anchor, anchor), (3 * TILE_F, 3 * TILE_R, COLS, 3, HEADS)).reshape(wide_size, 3, HEADS)
        near_max = stat_near[:, 0].T
        near_sum = stat_near[:, 1].T + 1.0
        near_spread = stat_near[:, 2].T
        pattern = lax.dynamic_slice(pattern_pad, (tile_a.astype(jnp.int32), tile_b.astype(jnp.int32), anchor, anchor), (3, 3, COLS // TILE_C, 27))
        pattern_tok = tile_tokens(pattern, TILE_F, TILE_R, TILE_C)
        reachable = jnp.einsum("eghxyz,fex,rgy,chz->frcegh", pattern_tok, key_table_f, key_table_r, key_column).reshape(slab_size, wide_size) > 0.5
        scores = jnp.einsum("khd,qhd->hkq", key_now, query_near) * scaling
        weights = jnp.exp(jnp.where(reachable[None], scores - near_max[:, None, :], -jnp.inf)) / near_sum[:, None, :]
        rounded = weights.astype(jnp.bfloat16)
        pushes = jnp.einsum("khd,qhd->hkq", value_now, grad_near)
        slopes = (weights * (pushes - near_spread[:, None, :])).astype(jnp.bfloat16)
        key_grad = (scaling * jnp.einsum("hkq,qhd->khd", slopes.astype(jnp.float32), query_near)).astype(jnp.bfloat16)
        value_grad = jnp.einsum("hkq,qhd->khd", rounded.astype(jnp.float32), grad_near).astype(jnp.bfloat16)
        return (key_grad.reshape(TILE_F, TILE_R, COLS, feat_width), value_grad.reshape(TILE_F, TILE_R, COLS, feat_width))

    key_blocks, value_blocks = lax.map(backward_slab, slab_ids)
    return attended, query_grad, to_grid(key_blocks), to_grid(value_blocks)
```

```python
import jax
import jax.numpy as jnp
from jax import lax
from jax.experimental import pallas as pl
from jax.experimental.pallas import tpu as pltpu
from jax.sharding import PartitionSpec as P

HEAD_DIM = 128
TILE = 192
SLOTS = 9
WIDE = SLOTS * TILE
SCALE = HEAD_DIM**-0.5
SCALE2 = SCALE * 1.4426950408889634
FAR = 1e30
VMEM_LIMIT = 48 * 1024 * 1024

VMEM = pl.BlockSpec(memory_space=pltpu.VMEM)
SMEM = pl.BlockSpec(memory_space=pltpu.SMEM)


def call(kernel, outs, in_specs, out_specs, scratch=()):
    return pl.pallas_call(
        kernel,
        out_shape=outs,
        in_specs=in_specs,
        out_specs=out_specs,
        scratch_shapes=list(scratch),
        compiler_params=pltpu.CompilerParams(vmem_limit_bytes=VMEM_LIMIT),
    )


def pair_swap(value, axis, parity):
    count = lax.axis_size(axis)
    pairs = []
    for low in range(parity, count - 1, 2):
        pairs += [(low, low + 1), (low + 1, low)]
    return lax.ppermute(value, axis, pairs)


def slot_steps(axis):
    near = 1 - 2 * (lax.axis_index(axis) % 2)
    return (0, near, -near)


def slot_offsets():
    return [(a, b) for a in slot_steps("frame") for b in slot_steps("row")]


def regroup_kernel(a_ref, b_ref, out_ref):
    out_ref[0 : 2 * TILE, :] = a_ref[...]
    out_ref[2 * TILE : 4 * TILE, :] = b_ref[...]


def gather_near(tiles, first_ref, second_ref):
    for slot, (ref, start) in enumerate(tiles):
        rows = slice(slot * TILE, (slot + 1) * TILE)
        first_ref[rows, :] = ref[start : start + TILE, :]
        second_ref[rows, :] = ref[start + TILE : start + 2 * TILE, :]


def store_sends(send_ref, firsts, seconds):
    heads = send_ref.shape[0]
    group, span = 8 // heads, TILE // heads
    row = lax.broadcasted_iota(jnp.int32, (TILE, TILE), 0)
    col = lax.broadcasted_iota(jnp.int32, (TILE, TILE), 1)
    block = jnp.zeros_like(row)
    for d in range(1, heads):
        block += (row >= d * span).astype(jnp.int32)
    inner = row - block * span
    shift = group.bit_length() - 1
    source = (inner >> shift) * 8 + block * group + (inner & (group - 1))
    order = (col == source).astype(jnp.bfloat16)
    joined = jnp.concatenate(firsts + seconds, axis=1)
    moved = jnp.dot(order, joined, preferred_element_type=jnp.float32).astype(jnp.bfloat16)
    feats = send_ref.shape[3]
    for k in range(heads):
        rows = slice(k * span, (k + 1) * span)
        send_ref[k, 0] = moved[rows, :feats]
        send_ref[k, 1] = moved[rows, feats:]


def assemble(got_ref, out_refs):
    heads, _, _, feats = got_ref.shape
    for k in range(heads):
        place = slice(k * feats, (k + 1) * feats)
        for i, out_ref in enumerate(out_refs):
            out_ref[:, :, place] = got_ref[k, i].reshape(out_ref.shape[:2] + (feats,))


def assemble_kernel(got_ref, *out_refs):
    assemble(got_ref, out_refs)


def query_kernel(
    pairs_s, pairs_v, own_qg, kv, kv_a, kv_b, kv_fb, kv_fa, corner_fb, corner_fa, *refs
):
    send_ref, stat_ref, key_ref, value_ref = refs
    frame, row = lax.axis_index("frame"), lax.axis_index("row")
    frames, rows = lax.axis_size("frame"), lax.axis_size("row")
    tiles = [(kv, 0), (kv_a, 0), (kv_b, 0)]
    tiles += [(kv_fa, 0), (corner_fa, 0), (corner_fa, 2 * TILE)]
    tiles += [(kv_fb, 0), (corner_fb, 0), (corner_fb, 2 * TILE)]
    gather_near(tiles, key_ref, value_ref)
    lane = lax.broadcasted_iota(jnp.int32, (1, WIDE), 1)
    bias = jnp.zeros((1, WIDE), jnp.float32)
    for slot, (a, b) in enumerate(slot_offsets()):
        bit = pairs_s[0, 0, 0, 9 * (a + 1) + 3 * (b + 1) + 1]
        inside = (frame + a >= 0) & (frame + a < frames) & (row + b >= 0) & (row + b < rows)
        level = jnp.where((bit == 1) & inside, 0.0, -FAR).astype(jnp.float32)
        here = (lane >= slot * TILE) & (lane < (slot + 1) * TILE)
        bias = jnp.where(here, level, bias)
    stat_lane = lax.broadcasted_iota(jnp.int32, (TILE, 128), 1)
    stats = jnp.zeros((TILE, 128), jnp.float32)
    count = own_qg.shape[1] // HEAD_DIM
    attended_parts, grad_parts = [], []
    for h in range(count):
        feat = slice(h * HEAD_DIM, (h + 1) * HEAD_DIM)
        query, grad = own_qg[0:TILE, feat], own_qg[TILE : 2 * TILE, feat]
        key, value = key_ref[:, feat], value_ref[:, feat]
        scores = lax.dot_general(
            query, key, (((1,), (1,)), ((), ())), preferred_element_type=jnp.float32
        )
        scores = scores * SCALE2 + bias
        top = jnp.max(scores, axis=1, keepdims=True)
        weights = jnp.exp2(scores - top)
        total = jnp.sum(weights, axis=1, keepdims=True)
        weights = weights * (1.0 / total)
        rounded = weights.astype(jnp.bfloat16)
        attended = jnp.dot(rounded, value, preferred_element_type=jnp.float32).astype(jnp.bfloat16)
        spread = jnp.sum(
            grad.astype(jnp.float32) * attended.astype(jnp.float32), axis=1, keepdims=True
        )
        pushes = lax.dot_general(
            grad, value, (((1,), (1,)), ((), ())), preferred_element_type=jnp.float32
        )
        slopes = (weights * (pushes - spread)).astype(jnp.bfloat16)
        query_grad = SCALE * jnp.dot(slopes, key, preferred_element_type=jnp.float32)
        attended_parts.append(attended)
        grad_parts.append(query_grad.astype(jnp.bfloat16))
        stats = jnp.where(stat_lane == h, top + jnp.log2(total), stats)
        stats = jnp.where(stat_lane == count + h, spread, stats)
    stat_ref[...] = stats.T[0:8, :]
    stat_ref[7:8, 0:27] = pairs_v[0, 0].astype(jnp.float32)
    store_sends(send_ref, attended_parts, grad_parts)


def key_kernel(kv, kv_fa, kv_fb, qg, qg_a, qg_b, st, st_a, st_b, *refs):
    own_ref, term_a_ref, term_b_ref, query_ref, grad_ref, stat_ref = refs
    count = kv.shape[1] // HEAD_DIM
    frame, frames = lax.axis_index("frame"), lax.axis_size("frame")
    gather_near([(qg, 0), (qg_a, 0), (qg_b, 0)], query_ref, grad_ref)
    lane = lax.broadcasted_iota(jnp.int32, (1, TILE), 1)
    level = lax.broadcasted_iota(jnp.int32, (8, TILE), 0)
    frame_steps = slot_steps("frame")
    for slot, (ref, b) in enumerate(zip((st, st_a, st_b), slot_steps("row"))):
        block = ref[...]
        for i, a in enumerate(frame_steps):
            index = 9 * (a + 1) + 3 * (1 - b) + 1
            bit = jnp.sum(jnp.where(lane == index, block[7:8, :], 0.0), axis=1, keepdims=True)
            inside = (frame + a >= 0) & (frame + a < frames)
            bit = bit * jnp.where(inside, 1.0, 0.0).astype(jnp.float32)
            closed = (level < count) & (bit < 0.5)
            stat_ref[i, :, slot * TILE : (slot + 1) * TILE] = jnp.where(closed, FAR, block)
    for h in range(count):
        feat = slice(h * HEAD_DIM, (h + 1) * HEAD_DIM)
        query, grad = query_ref[:, feat], grad_ref[:, feat]
        for i, (kv_ref, out_ref) in enumerate(
            ((kv, own_ref), (kv_fa, term_a_ref), (kv_fb, term_b_ref))
        ):
            key, value = kv_ref[0:TILE, feat], kv_ref[TILE : 2 * TILE, feat]
            scores = lax.dot_general(
                key, query, (((1,), (1,)), ((), ())), preferred_element_type=jnp.float32
            )
            weights = jnp.exp2(scores * SCALE2 - stat_ref[i, h : h + 1, :])
            rounded = weights.astype(jnp.bfloat16)
            value_grad = jnp.dot(rounded, grad, preferred_element_type=jnp.float32)
            pushes = lax.dot_general(
                value, grad, (((1,), (1,)), ((), ())), preferred_element_type=jnp.float32
            )
            spread = stat_ref[i, count + h : count + h + 1, :]
            slopes = (weights * (pushes - spread)).astype(jnp.bfloat16)
            key_grad = SCALE * jnp.dot(slopes, query, preferred_element_type=jnp.float32)
            out_ref[0:TILE, feat] = key_grad.astype(out_ref.dtype)
            out_ref[TILE : 2 * TILE, feat] = value_grad.astype(out_ref.dtype)


def fold_kernel(own_ref, got_a, got_b, send_ref):
    total = own_ref[...] + got_a[...].astype(jnp.float32) + got_b[...].astype(jnp.float32)
    total = total.astype(jnp.bfloat16)
    store_sends(send_ref, [total[0:TILE]], [total[TILE : 2 * TILE]])


def after(value, *others):
    return lax.optimization_barrier((value,) + others)[0]


def stacked(first, second):
    rows = first.shape[0]
    low = jnp.pad(first, ((0, rows), (0, 0)), constant_values=-jnp.inf)
    return jnp.maximum(low, jnp.pad(second, ((rows, 0), (0, 0)), constant_values=-jnp.inf))


def body(queries, key_tokens, value_tokens, grad_out, tile_pairs):
    frames_dev, rows_dev, columns, feats = queries.shape
    heads = lax.axis_size("head")
    bf16, f32 = jnp.bfloat16, jnp.float32
    flat = [x.reshape(TILE, feats) for x in (key_tokens, value_tokens, queries, grad_out)]

    kv = stacked(flat[0], flat[1])
    qg = stacked(flat[2], flat[3])
    kv_a, kv_b = pair_swap(kv, "row", 0), pair_swap(kv, "row", 1)
    kv_fb, kv_fa = pair_swap(kv, "frame", 1), pair_swap(kv, "frame", 0)
    rows = call(regroup_kernel, jax.ShapeDtypeStruct((4 * TILE, feats), bf16), [VMEM] * 2, VMEM)(
        kv_a, kv_b
    )
    rows = after(rows, kv_fb, kv_fa)
    corner_fb, corner_fa = pair_swap(rows, "frame", 1), pair_swap(rows, "frame", 0)
    qg_late = after(qg, kv_fb, kv_fa)
    qg_a, qg_b = pair_swap(qg_late, "row", 0), pair_swap(qg_late, "row", 1)

    send_shape = jax.ShapeDtypeStruct((heads, 2, TILE // heads, feats), bf16)
    near = pltpu.VMEM((WIDE, feats), bf16)
    sent_q, stat = call(
        query_kernel,
        (send_shape, jax.ShapeDtypeStruct((8, TILE), f32)),
        [SMEM] + [VMEM] * 9,
        (VMEM, VMEM),
        [near, near],
    )(tile_pairs, tile_pairs, qg, kv, kv_a, kv_b, kv_fb, kv_fa, corner_fb, corner_fa)
    st_a, st_b = pair_swap(stat, "row", 0), pair_swap(stat, "row", 1)

    row_near = pltpu.VMEM((3 * TILE, feats), bf16)
    term = jax.ShapeDtypeStruct((2 * TILE, feats), bf16)
    own, term_a, term_b = call(
        key_kernel,
        (jax.ShapeDtypeStruct((2 * TILE, feats), f32), term, term),
        [VMEM] * 9,
        (VMEM,) * 3,
        [row_near, row_near, pltpu.VMEM((3, 8, 3 * TILE), f32)],
    )(kv, kv_fa, kv_fb, qg, qg_a, qg_b, stat, st_a, st_b)
    got_b, got_a = pair_swap(term_b, "frame", 1), pair_swap(term_a, "frame", 0)
    sent_k = call(fold_kernel, send_shape, [VMEM] * 3, VMEM)(own, got_b, got_a)

    out = jax.ShapeDtypeStruct((frames_dev * rows_dev, columns // heads, heads * feats), bf16)
    outs = []
    for sent in (after(sent_q, own), sent_k):
        got = lax.all_to_all(sent, "head", split_axis=0, concat_axis=0, tiled=True)
        outs += call(assemble_kernel, (out, out), [VMEM], (VMEM, VMEM))(got)
    return tuple(x.reshape((frames_dev, rows_dev) + out.shape[1:]) for x in outs)


def solution(mesh):
    inputs = P("frame", "row", None, "head")
    outputs = P("frame", "row", "head", None)
    return jax.shard_map(
        body,
        mesh=mesh,
        in_specs=(inputs,) * 4 + (P("frame", "row", None, None),),
        out_specs=(outputs,) * 4,
        check_vma=False,
    )
```

```python
import jax
import jax.numpy as jnp
from jax import lax
from jax.experimental import pallas as pl
from jax.experimental.pallas import tpu as pltpu
from jax.sharding import PartitionSpec as P

HEAD_DIM = 128
TILE = 192
SLOTS = 9
WIDE = SLOTS * TILE
SCALE = HEAD_DIM**-0.5
SCALE2 = SCALE * 1.4426950408889634
FAR = 1e30
VMEM_LIMIT = 48 * 1024 * 1024

VMEM = pl.BlockSpec(memory_space=pltpu.VMEM)
SMEM = pl.BlockSpec(memory_space=pltpu.SMEM)


def call(kernel, outs, in_specs, out_specs, scratch=()):
    return pl.pallas_call(
        kernel,
        out_shape=outs,
        in_specs=in_specs,
        out_specs=out_specs,
        scratch_shapes=list(scratch),
        compiler_params=pltpu.CompilerParams(vmem_limit_bytes=VMEM_LIMIT),
    )


def pair_swap(value, axis, parity):
    count = lax.axis_size(axis)
    pairs = []
    for low in range(parity, count - 1, 2):
        pairs += [(low, low + 1), (low + 1, low)]
    return lax.ppermute(value, axis, pairs)


def slot_steps(axis):
    near = 1 - 2 * (lax.axis_index(axis) % 2)
    return (0, near, -near)


def slot_offsets():
    return [(a, b) for a in slot_steps("frame") for b in slot_steps("row")]


def regroup_kernel(own_ref, a_ref, b_ref, out_ref):
    for i, ref in enumerate((own_ref, a_ref, b_ref)):
        out_ref[2 * TILE * i : 2 * TILE * (i + 1), :] = ref[...]


def gather_near(tiles, first_ref, second_ref):
    for slot, (ref, start) in enumerate(tiles):
        rows = slice(slot * TILE, (slot + 1) * TILE)
        first_ref[rows, :] = ref[start : start + TILE, :]
        second_ref[rows, :] = ref[start + TILE : start + 2 * TILE, :]


def store_sends(send_ref, firsts, seconds):
    heads = send_ref.shape[0]
    group, span = 8 // heads, TILE // heads
    row = lax.broadcasted_iota(jnp.int32, (TILE, TILE), 0)
    col = lax.broadcasted_iota(jnp.int32, (TILE, TILE), 1)
    block = jnp.zeros_like(row)
    for d in range(1, heads):
        block += (row >= d * span).astype(jnp.int32)
    inner = row - block * span
    shift = group.bit_length() - 1
    source = (inner >> shift) * 8 + block * group + (inner & (group - 1))
    order = (col == source).astype(jnp.bfloat16)
    joined = jnp.concatenate(firsts + seconds, axis=1)
    moved = jnp.dot(order, joined, preferred_element_type=jnp.float32).astype(jnp.bfloat16)
    feats = send_ref.shape[3]
    for k in range(heads):
        rows = slice(k * span, (k + 1) * span)
        send_ref[k, 0] = moved[rows, :feats]
        send_ref[k, 1] = moved[rows, feats:]


def assemble(got_ref, out_refs):
    heads, _, _, feats = got_ref.shape
    for k in range(heads):
        place = slice(k * feats, (k + 1) * feats)
        for i, out_ref in enumerate(out_refs):
            out_ref[:, :, place] = got_ref[k, i].reshape(out_ref.shape[:2] + (feats,))


def assemble_kernel(got_ref, *out_refs):
    assemble(got_ref, out_refs)


def query_kernel(
    pairs_s, pairs_v, own_qg, kv, kv_fb, kv_fa, send_ref, stat_ref, key_ref, value_ref
):
    frame, row = lax.axis_index("frame"), lax.axis_index("row")
    frames, rows = lax.axis_size("frame"), lax.axis_size("row")
    tiles = [(ref, 2 * TILE * i) for ref in (kv, kv_fa, kv_fb) for i in range(3)]
    gather_near(tiles, key_ref, value_ref)
    lane = lax.broadcasted_iota(jnp.int32, (1, WIDE), 1)
    bias = jnp.zeros((1, WIDE), jnp.float32)
    for slot, (a, b) in enumerate(slot_offsets()):
        bit = pairs_s[0, 0, 0, 9 * (a + 1) + 3 * (b + 1) + 1]
        inside = (frame + a >= 0) & (frame + a < frames) & (row + b >= 0) & (row + b < rows)
        level = jnp.where((bit == 1) & inside, 0.0, -FAR).astype(jnp.float32)
        here = (lane >= slot * TILE) & (lane < (slot + 1) * TILE)
        bias = jnp.where(here, level, bias)
    stat_lane = lax.broadcasted_iota(jnp.int32, (TILE, 128), 1)
    stats = jnp.zeros((TILE, 128), jnp.float32)
    count = own_qg.shape[1] // HEAD_DIM
    attended_parts, grad_parts = [], []
    for h in range(count):
        feat = slice(h * HEAD_DIM, (h + 1) * HEAD_DIM)
        query, grad = own_qg[0:TILE, feat], own_qg[TILE : 2 * TILE, feat]
        key, value = key_ref[:, feat], value_ref[:, feat]
        scores = lax.dot_general(
            query, key, (((1,), (1,)), ((), ())), preferred_element_type=jnp.float32
        )
        scores = scores * SCALE2 + bias
        top = jnp.max(scores, axis=1, keepdims=True)
        weights = jnp.exp2(scores - top)
        total = jnp.sum(weights, axis=1, keepdims=True)
        weights = weights * (1.0 / total)
        rounded = weights.astype(jnp.bfloat16)
        attended = jnp.dot(rounded, value, preferred_element_type=jnp.float32).astype(jnp.bfloat16)
        spread = jnp.sum(
            grad.astype(jnp.float32) * attended.astype(jnp.float32), axis=1, keepdims=True
        )
        pushes = lax.dot_general(
            grad, value, (((1,), (1,)), ((), ())), preferred_element_type=jnp.float32
        )
        slopes = (weights * (pushes - spread)).astype(jnp.bfloat16)
        query_grad = SCALE * jnp.dot(slopes, key, preferred_element_type=jnp.float32)
        attended_parts.append(attended)
        grad_parts.append(query_grad.astype(jnp.bfloat16))
        stats = jnp.where(stat_lane == h, top + jnp.log2(total), stats)
        stats = jnp.where(stat_lane == count + h, spread, stats)
    stat_ref[...] = stats.T[0:8, :]
    stat_ref[7:8, 0:27] = pairs_v[0, 0].astype(jnp.float32)
    store_sends(send_ref, attended_parts, grad_parts)


def key_kernel(sides, *refs):
    kvs, refs = refs[: len(sides)], refs[len(sides) :]
    (qg, qg_a, qg_b, st, st_a, st_b), refs = refs[:6], refs[6:]
    outs, (query_ref, grad_ref, stat_ref) = refs[: len(sides)], refs[len(sides) :]
    count = qg.shape[1] // HEAD_DIM
    frame, frames = lax.axis_index("frame"), lax.axis_size("frame")
    gather_near([(qg, 0), (qg_a, 0), (qg_b, 0)], query_ref, grad_ref)
    lane = lax.broadcasted_iota(jnp.int32, (1, TILE), 1)
    level = lax.broadcasted_iota(jnp.int32, (8, TILE), 0)
    frame_steps = [slot_steps("frame")[side] for side in sides]
    for slot, (ref, b) in enumerate(zip((st, st_a, st_b), slot_steps("row"))):
        block = ref[...]
        for i, a in enumerate(frame_steps):
            index = 9 * (a + 1) + 3 * (1 - b) + 1
            bit = jnp.sum(jnp.where(lane == index, block[7:8, :], 0.0), axis=1, keepdims=True)
            inside = (frame + a >= 0) & (frame + a < frames)
            bit = bit * jnp.where(inside, 1.0, 0.0).astype(jnp.float32)
            closed = (level < count) & (bit < 0.5)
            stat_ref[i, :, slot * TILE : (slot + 1) * TILE] = jnp.where(closed, FAR, block)
    for h in range(count):
        feat = slice(h * HEAD_DIM, (h + 1) * HEAD_DIM)
        query, grad = query_ref[:, feat], grad_ref[:, feat]
        for i, (kv_ref, out_ref) in enumerate(zip(kvs, outs)):
            key, value = kv_ref[0:TILE, feat], kv_ref[TILE : 2 * TILE, feat]
            scores = lax.dot_general(
                key, query, (((1,), (1,)), ((), ())), preferred_element_type=jnp.float32
            )
            weights = jnp.exp2(scores * SCALE2 - stat_ref[i, h : h + 1, :])
            rounded = weights.astype(jnp.bfloat16)
            value_grad = jnp.dot(rounded, grad, preferred_element_type=jnp.float32)
            pushes = lax.dot_general(
                value, grad, (((1,), (1,)), ((), ())), preferred_element_type=jnp.float32
            )
            spread = stat_ref[i, count + h : count + h + 1, :]
            slopes = (weights * (pushes - spread)).astype(jnp.bfloat16)
            key_grad = SCALE * jnp.dot(slopes, query, preferred_element_type=jnp.float32)
            out_ref[0:TILE, feat] = key_grad.astype(out_ref.dtype)
            out_ref[TILE : 2 * TILE, feat] = value_grad.astype(out_ref.dtype)


def fold_kernel(own_ref, got_a, got_b, send_ref):
    total = own_ref[...] + got_a[...].astype(jnp.float32) + got_b[...].astype(jnp.float32)
    total = total.astype(jnp.bfloat16)
    store_sends(send_ref, [total[0:TILE]], [total[TILE : 2 * TILE]])


def after(value, *others):
    return lax.optimization_barrier((value,) + others)[0]


def stacked(first, second):
    rows = first.shape[0]
    low = jnp.pad(first, ((0, rows), (0, 0)), constant_values=-jnp.inf)
    return jnp.maximum(low, jnp.pad(second, ((rows, 0), (0, 0)), constant_values=-jnp.inf))


def body(queries, key_tokens, value_tokens, grad_out, tile_pairs):
    frames_dev, rows_dev, columns, feats = queries.shape
    heads = lax.axis_size("head")
    bf16, f32 = jnp.bfloat16, jnp.float32
    flat = [x.reshape(TILE, feats) for x in (key_tokens, value_tokens, queries, grad_out)]

    own_kv = stacked(flat[0], flat[1])
    kv_a, kv_b = pair_swap(own_kv, "row", 0), pair_swap(own_kv, "row", 1)
    triple = jax.ShapeDtypeStruct((6 * TILE, feats), bf16)
    kv = call(regroup_kernel, triple, [VMEM] * 3, VMEM)(own_kv, kv_a, kv_b)
    kv_fb, kv_fa = pair_swap(kv, "frame", 1), pair_swap(kv, "frame", 0)
    qg = stacked(flat[2], flat[3])
    qg_late = after(qg, kv)
    qg_a, qg_b = pair_swap(qg_late, "row", 0), pair_swap(qg_late, "row", 1)

    send_shape = jax.ShapeDtypeStruct((heads, 2, TILE // heads, feats), bf16)
    near = pltpu.VMEM((WIDE, feats), bf16)
    sent_q, stat = call(
        query_kernel,
        (send_shape, jax.ShapeDtypeStruct((8, TILE), f32)),
        [SMEM] + [VMEM] * 5,
        (VMEM, VMEM),
        [near, near],
    )(tile_pairs, tile_pairs, qg, kv, kv_fb, kv_fa)
    st_a, st_b = pair_swap(stat, "row", 0), pair_swap(stat, "row", 1)

    def terms(sides, kinds, *kvs):
        row_near = pltpu.VMEM((3 * TILE, feats), bf16)
        return call(
            lambda *refs: key_kernel(sides, *refs),
            [jax.ShapeDtypeStruct((2 * TILE, feats), kind) for kind in kinds],
            [VMEM] * (len(sides) + 6),
            [VMEM] * len(sides),
            [row_near, row_near, pltpu.VMEM((len(sides), 8, 3 * TILE), f32)],
        )(*kvs, qg, qg_a, qg_b, stat, st_a, st_b)

    (term_b,) = terms((2,), (bf16,), kv_fb)
    got_b = pair_swap(term_b, "frame", 1)
    term_a, own = terms((1, 0), (bf16, f32), kv_fa, after(own_kv, term_b))
    got_a = pair_swap(term_a, "frame", 0)
    sent_k = call(fold_kernel, send_shape, [VMEM] * 3, VMEM)(own, got_b, got_a)

    out = jax.ShapeDtypeStruct((frames_dev * rows_dev, columns // heads, heads * feats), bf16)
    outs = []
    for sent in (after(sent_q, st_a, st_b), sent_k):
        got = lax.all_to_all(sent, "head", split_axis=0, concat_axis=0, tiled=True)
        outs += call(assemble_kernel, (out, out), [VMEM], (VMEM, VMEM))(got)
    return tuple(x.reshape((frames_dev, rows_dev) + out.shape[1:]) for x in outs)


def solution(mesh):
    inputs = P("frame", "row", None, "head")
    outputs = P("frame", "row", "head", None)
    return jax.shard_map(
        body,
        mesh=mesh,
        in_specs=(inputs,) * 4 + (P("frame", "row", None, None),),
        out_specs=(outputs,) * 4,
        check_vma=False,
    )
```

```python
import jax
import jax.numpy as jnp
from jax import lax
from jax.experimental import pallas as pl
from jax.experimental.pallas import tpu as pltpu
from jax.sharding import PartitionSpec as P

HEAD_DIM = 128
TILE = 192
SLOTS = 9
WIDE = SLOTS * TILE
SCALE = HEAD_DIM**-0.5
SCALE2 = SCALE * 1.4426950408889634
FAR = 1e30
VMEM_LIMIT = 48 * 1024 * 1024

VMEM = pl.BlockSpec(memory_space=pltpu.VMEM)
SMEM = pl.BlockSpec(memory_space=pltpu.SMEM)


def call(kernel, outs, in_specs, out_specs, scratch=()):
    return pl.pallas_call(
        kernel,
        out_shape=outs,
        in_specs=in_specs,
        out_specs=out_specs,
        scratch_shapes=list(scratch),
        compiler_params=pltpu.CompilerParams(vmem_limit_bytes=VMEM_LIMIT),
    )


def pair_swap(value, axis, parity):
    count = lax.axis_size(axis)
    pairs = []
    for low in range(parity, count - 1, 2):
        pairs += [(low, low + 1), (low + 1, low)]
    return lax.ppermute(value, axis, pairs)


def slot_steps(axis):
    near = 1 - 2 * (lax.axis_index(axis) % 2)
    return (0, near, -near)


def slot_offsets():
    return [(a, b) for a in slot_steps("frame") for b in slot_steps("row")]


def regroup_kernel(a_ref, b_ref, out_ref):
    out_ref[0 : 2 * TILE, :] = a_ref[...]
    out_ref[2 * TILE : 4 * TILE, :] = b_ref[...]


def gather_near(tiles, first_ref, second_ref):
    for slot, (ref, start) in enumerate(tiles):
        rows = slice(slot * TILE, (slot + 1) * TILE)
        first_ref[rows, :] = ref[start : start + TILE, :]
        second_ref[rows, :] = ref[start + TILE : start + 2 * TILE, :]


def column_blocks(firsts, seconds, heads):
    group, span = 8 // heads, TILE // heads
    me = lax.axis_index("head")
    row = lax.broadcasted_iota(jnp.int32, (TILE, TILE), 0)
    col = lax.broadcasted_iota(jnp.int32, (TILE, TILE), 1)
    block = jnp.zeros_like(row)
    for d in range(1, heads):
        block += (row >= d * span).astype(jnp.int32)
    inner = row - block * span
    shift = group.bit_length() - 1
    source = (inner >> shift) * 8 + (block ^ me) * group + (inner & (group - 1))
    order = (col == source).astype(jnp.bfloat16)
    joined = jnp.concatenate(firsts + seconds, axis=1)
    moved = jnp.dot(order, joined, preferred_element_type=jnp.float32).astype(jnp.bfloat16)
    feats = joined.shape[1] // 2
    return [
        [moved[k * span : (k + 1) * span, i * feats : (i + 1) * feats] for i in range(2)]
        for k in range(heads)
    ]


def near_heads(heads):
    return [k for k in range(heads) if k != heads // 2]


def assemble_kernel(heads, far_q, far_k, *refs):
    near_refs, out_refs = refs[: heads - 1], refs[heads - 1 :]
    feats = far_q.shape[2]
    me = lax.axis_index("head")

    def put(k, i, rows):
        place = pl.ds(pl.multiple_of((me ^ k) * feats, HEAD_DIM), feats)
        out_refs[i][:, :, place] = rows.reshape(out_refs[i].shape[:2] + (feats,))

    for i in range(2):
        put(heads // 2, i, far_q[i])
        put(heads // 2, 2 + i, far_k[i])
    for k, ref in zip(near_heads(heads), near_refs):
        for i in range(4):
            put(k, i, ref[i])


def query_kernel(
    heads, pairs_s, pairs_v, own_qg, kv, kv_a, kv_b, kv_fb, kv_fa, corner_fb, corner_fa, *refs
):
    far_ref, near_ref, stat_ref, key_ref, value_ref = refs
    frame, row = lax.axis_index("frame"), lax.axis_index("row")
    frames, rows = lax.axis_size("frame"), lax.axis_size("row")
    tiles = [(kv, 0), (kv_a, 0), (kv_b, 0)]
    tiles += [(kv_fa, 0), (corner_fa, 0), (corner_fa, 2 * TILE)]
    tiles += [(kv_fb, 0), (corner_fb, 0), (corner_fb, 2 * TILE)]
    gather_near(tiles, key_ref, value_ref)
    lane = lax.broadcasted_iota(jnp.int32, (1, WIDE), 1)
    bias = jnp.zeros((1, WIDE), jnp.float32)
    for slot, (a, b) in enumerate(slot_offsets()):
        bit = pairs_s[0, 0, 0, 9 * (a + 1) + 3 * (b + 1) + 1]
        inside = (frame + a >= 0) & (frame + a < frames) & (row + b >= 0) & (row + b < rows)
        level = jnp.where((bit == 1) & inside, 0.0, -FAR).astype(jnp.float32)
        here = (lane >= slot * TILE) & (lane < (slot + 1) * TILE)
        bias = jnp.where(here, level, bias)
    stat_lane = lax.broadcasted_iota(jnp.int32, (TILE, 128), 1)
    stats = jnp.zeros((TILE, 128), jnp.float32)
    count = own_qg.shape[1] // HEAD_DIM
    attended_parts, grad_parts = [], []
    for h in range(count):
        feat = slice(h * HEAD_DIM, (h + 1) * HEAD_DIM)
        query, grad = own_qg[0:TILE, feat], own_qg[TILE : 2 * TILE, feat]
        key, value = key_ref[:, feat], value_ref[:, feat]
        scores = lax.dot_general(
            query, key, (((1,), (1,)), ((), ())), preferred_element_type=jnp.float32
        )
        scores = scores * SCALE2 + bias
        top = jnp.max(scores, axis=1, keepdims=True)
        weights = jnp.exp2(scores - top)
        total = jnp.sum(weights, axis=1, keepdims=True)
        weights = weights * (1.0 / total)
        rounded = weights.astype(jnp.bfloat16)
        attended = jnp.dot(rounded, value, preferred_element_type=jnp.float32).astype(jnp.bfloat16)
        spread = jnp.sum(
            grad.astype(jnp.float32) * attended.astype(jnp.float32), axis=1, keepdims=True
        )
        pushes = lax.dot_general(
            grad, value, (((1,), (1,)), ((), ())), preferred_element_type=jnp.float32
        )
        slopes = (weights * (pushes - spread)).astype(jnp.bfloat16)
        query_grad = SCALE * jnp.dot(slopes, key, preferred_element_type=jnp.float32)
        attended_parts.append(attended)
        grad_parts.append(query_grad.astype(jnp.bfloat16))
        stats = jnp.where(stat_lane == h, top + jnp.log2(total), stats)
        stats = jnp.where(stat_lane == count + h, spread, stats)
    stat_ref[...] = stats.T[0:8, :]
    stat_ref[7:8, 0:27] = pairs_v[0, 0].astype(jnp.float32)
    blocks = column_blocks(attended_parts, grad_parts, heads)
    for i in range(2):
        far_ref[i] = blocks[heads // 2][i]
        for at, k in enumerate(near_heads(heads)):
            near_ref[at, i] = blocks[k][i]


def key_kernel(kv, kv_fa, kv_fb, qg, qg_a, qg_b, st, st_a, st_b, *refs):
    own_ref, term_a_ref, term_b_ref, query_ref, grad_ref, stat_ref = refs
    count = kv.shape[1] // HEAD_DIM
    frame, frames = lax.axis_index("frame"), lax.axis_size("frame")
    gather_near([(qg, 0), (qg_a, 0), (qg_b, 0)], query_ref, grad_ref)
    lane = lax.broadcasted_iota(jnp.int32, (1, TILE), 1)
    level = lax.broadcasted_iota(jnp.int32, (8, TILE), 0)
    frame_steps = slot_steps("frame")
    for slot, (ref, b) in enumerate(zip((st, st_a, st_b), slot_steps("row"))):
        block = ref[...]
        for i, a in enumerate(frame_steps):
            index = 9 * (a + 1) + 3 * (1 - b) + 1
            bit = jnp.sum(jnp.where(lane == index, block[7:8, :], 0.0), axis=1, keepdims=True)
            inside = (frame + a >= 0) & (frame + a < frames)
            bit = bit * jnp.where(inside, 1.0, 0.0).astype(jnp.float32)
            closed = (level < count) & (bit < 0.5)
            stat_ref[i, :, slot * TILE : (slot + 1) * TILE] = jnp.where(closed, FAR, block)
    for h in range(count):
        feat = slice(h * HEAD_DIM, (h + 1) * HEAD_DIM)
        query, grad = query_ref[:, feat], grad_ref[:, feat]
        for i, (kv_ref, out_ref) in enumerate(
            ((kv, own_ref), (kv_fa, term_a_ref), (kv_fb, term_b_ref))
        ):
            key, value = kv_ref[0:TILE, feat], kv_ref[TILE : 2 * TILE, feat]
            scores = lax.dot_general(
                key, query, (((1,), (1,)), ((), ())), preferred_element_type=jnp.float32
            )
            weights = jnp.exp2(scores * SCALE2 - stat_ref[i, h : h + 1, :])
            rounded = weights.astype(jnp.bfloat16)
            value_grad = jnp.dot(rounded, grad, preferred_element_type=jnp.float32)
            pushes = lax.dot_general(
                value, grad, (((1,), (1,)), ((), ())), preferred_element_type=jnp.float32
            )
            spread = stat_ref[i, count + h : count + h + 1, :]
            slopes = (weights * (pushes - spread)).astype(jnp.bfloat16)
            key_grad = SCALE * jnp.dot(slopes, query, preferred_element_type=jnp.float32)
            out_ref[0:TILE, feat] = key_grad.astype(out_ref.dtype)
            out_ref[TILE : 2 * TILE, feat] = value_grad.astype(out_ref.dtype)


def fold_kernel(heads, own_ref, got_a, got_b, near_q, far_ref, *near_refs):
    total = own_ref[...] + got_a[...].astype(jnp.float32) + got_b[...].astype(jnp.float32)
    total = total.astype(jnp.bfloat16)
    blocks = column_blocks([total[0:TILE]], [total[TILE : 2 * TILE]], heads)
    for i in range(2):
        far_ref[i] = blocks[heads // 2][i]
        for at, (k, ref) in enumerate(zip(near_heads(heads), near_refs)):
            ref[i] = near_q[at, i]
            ref[2 + i] = blocks[k][i]


def after(value, *others):
    return lax.optimization_barrier((value,) + others)[0]


def head_swap(value, k):
    count = lax.axis_size("head")
    return lax.ppermute(value, "head", [(i, i ^ k) for i in range(count)]) if k else value


def stacked(first, second):
    rows = first.shape[0]
    low = jnp.pad(first, ((0, rows), (0, 0)), constant_values=-jnp.inf)
    return jnp.maximum(low, jnp.pad(second, ((rows, 0), (0, 0)), constant_values=-jnp.inf))


def body(queries, key_tokens, value_tokens, grad_out, tile_pairs):
    frames_dev, rows_dev, columns, feats = queries.shape
    heads = lax.axis_size("head")
    bf16, f32 = jnp.bfloat16, jnp.float32
    flat = [x.reshape(TILE, feats) for x in (key_tokens, value_tokens, queries, grad_out)]

    kv = stacked(flat[0], flat[1])
    qg = stacked(flat[2], flat[3])
    kv_a, kv_b = pair_swap(kv, "row", 0), pair_swap(kv, "row", 1)
    kv_fb, kv_fa = pair_swap(kv, "frame", 1), pair_swap(kv, "frame", 0)
    rows = call(regroup_kernel, jax.ShapeDtypeStruct((4 * TILE, feats), bf16), [VMEM] * 2, VMEM)(
        kv_a, kv_b
    )
    rows = after(rows, kv_fb, kv_fa)
    corner_fb, corner_fa = pair_swap(rows, "frame", 1), pair_swap(rows, "frame", 0)
    qg_late = after(qg, kv_fb, kv_fa)
    qg_a, qg_b = pair_swap(qg_late, "row", 0), pair_swap(qg_late, "row", 1)

    span = TILE // heads
    pair, four = (jax.ShapeDtypeStruct((n, span, feats), bf16) for n in (2, 4))
    near_shape = jax.ShapeDtypeStruct((heads - 1, 2, span, feats), bf16)
    near = pltpu.VMEM((WIDE, feats), bf16)
    far_q, near_q, stat = call(
        lambda *refs: query_kernel(heads, *refs),
        (pair, near_shape, jax.ShapeDtypeStruct((8, TILE), f32)),
        [SMEM] + [VMEM] * 9,
        (VMEM,) * 3,
        [near, near],
    )(tile_pairs, tile_pairs, qg, kv, kv_a, kv_b, kv_fb, kv_fa, corner_fb, corner_fa)
    st_a, st_b = pair_swap(stat, "row", 0), pair_swap(stat, "row", 1)
    got_far_q = head_swap(far_q, heads // 2)

    row_near = pltpu.VMEM((3 * TILE, feats), bf16)
    term = jax.ShapeDtypeStruct((2 * TILE, feats), bf16)
    own, term_a, term_b = call(
        key_kernel,
        (jax.ShapeDtypeStruct((2 * TILE, feats), f32), term, term),
        [VMEM] * 9,
        (VMEM,) * 3,
        [row_near, row_near, pltpu.VMEM((3, 8, 3 * TILE), f32)],
    )(after(kv, got_far_q), kv_fa, kv_fb, qg, qg_a, qg_b, stat, st_a, st_b)
    got_b, got_a = pair_swap(term_b, "frame", 1), pair_swap(term_a, "frame", 0)
    far_k, *near_k = call(
        lambda *refs: fold_kernel(heads, *refs),
        [pair] + [four] * (heads - 1),
        [VMEM] * 4,
        [VMEM] * heads,
    )(own, got_b, got_a, near_q)
    got_far_k = head_swap(far_k, heads // 2)
    got_near = [head_swap(sent, k) for k, sent in zip(near_heads(heads), near_k)]

    out = jax.ShapeDtypeStruct((frames_dev * rows_dev, columns // heads, heads * feats), bf16)
    outs = call(
        lambda *refs: assemble_kernel(heads, *refs),
        [out] * 4,
        [VMEM] * (heads + 1),
        [VMEM] * 4,
    )(got_far_q, got_far_k, *got_near)
    return tuple(x.reshape((frames_dev, rows_dev) + out.shape[1:]) for x in outs)


def solution(mesh):
    inputs = P("frame", "row", None, "head")
    outputs = P("frame", "row", "head", None)
    return jax.shard_map(
        body,
        mesh=mesh,
        in_specs=(inputs,) * 4 + (P("frame", "row", None, None),),
        out_specs=(outputs,) * 4,
        check_vma=False,
    )
```

```python
import jax
import jax.numpy as jnp
from jax import lax
from jax.experimental import pallas as pl
from jax.experimental.pallas import tpu as pltpu
from jax.sharding import PartitionSpec as P

HEAD_DIM = 128
TILE = 192
SLOTS = 9
WIDE = SLOTS * TILE
SCALE = HEAD_DIM**-0.5
SCALE2 = SCALE * 1.4426950408889634
FAR = 1e30
VMEM_LIMIT = 48 * 1024 * 1024

VMEM = pl.BlockSpec(memory_space=pltpu.VMEM)
SMEM = pl.BlockSpec(memory_space=pltpu.SMEM)


def call(kernel, outs, in_specs, out_specs, scratch=()):
    return pl.pallas_call(
        kernel,
        out_shape=outs,
        in_specs=in_specs,
        out_specs=out_specs,
        scratch_shapes=list(scratch),
        compiler_params=pltpu.CompilerParams(vmem_limit_bytes=VMEM_LIMIT),
    )


def pair_swap(value, axis, parity):
    count = lax.axis_size(axis)
    pairs = []
    for low in range(parity, count - 1, 2):
        pairs += [(low, low + 1), (low + 1, low)]
    return lax.ppermute(value, axis, pairs)


def slot_steps(axis):
    near = 1 - 2 * (lax.axis_index(axis) % 2)
    return (0, near, -near)


def slot_offsets():
    return [(a, b) for a in slot_steps("frame") for b in slot_steps("row")]


def regroup_kernel(a_ref, b_ref, out_ref):
    out_ref[0 : 2 * TILE, :] = a_ref[...]
    out_ref[2 * TILE : 4 * TILE, :] = b_ref[...]


def gather_near(tiles, first_ref, second_ref):
    for slot, (ref, start) in enumerate(tiles):
        rows = slice(slot * TILE, (slot + 1) * TILE)
        first_ref[rows, :] = ref[start : start + TILE, :]
        second_ref[rows, :] = ref[start + TILE : start + 2 * TILE, :]


def column_blocks(firsts, seconds, heads):
    group, span = 8 // heads, TILE // heads
    me = lax.axis_index("head")
    row = lax.broadcasted_iota(jnp.int32, (TILE, TILE), 0)
    col = lax.broadcasted_iota(jnp.int32, (TILE, TILE), 1)
    block = jnp.zeros_like(row)
    for d in range(1, heads):
        block += (row >= d * span).astype(jnp.int32)
    inner = row - block * span
    shift = group.bit_length() - 1
    source = (inner >> shift) * 8 + (block ^ me) * group + (inner & (group - 1))
    order = (col == source).astype(jnp.bfloat16)
    joined = jnp.concatenate(firsts + seconds, axis=1)
    moved = jnp.dot(order, joined, preferred_element_type=jnp.float32).astype(jnp.bfloat16)
    feats = joined.shape[1] // 2
    return [
        [moved[k * span : (k + 1) * span, i * feats : (i + 1) * feats] for i in range(2)]
        for k in range(heads)
    ]


def near_heads(heads):
    return [k for k in range(heads) if k != heads // 2]


def assemble_kernel(heads, far_q, far_k, *refs):
    near_refs, out_refs = refs[: heads - 1], refs[heads - 1 :]
    feats = far_q.shape[2]
    me = lax.axis_index("head")

    def put(k, i, rows):
        place = pl.ds(pl.multiple_of((me ^ k) * feats, HEAD_DIM), feats)
        out_refs[i][:, :, place] = rows.reshape(out_refs[i].shape[:2] + (feats,))

    for i in range(2):
        put(heads // 2, i, far_q[i])
        put(heads // 2, 2 + i, far_k[i])
    for k, ref in zip(near_heads(heads), near_refs):
        for i in range(4):
            put(k, i, ref[i])


def query_kernel(
    pairs_s, pairs_v, own_qg, kv, kv_a, kv_b, kv_fb, kv_fa, corner_fb, corner_fa, *refs
):
    attended_ref, stat_ref, column_ref, bias_ref, key_ref, value_ref = refs
    frame, row = lax.axis_index("frame"), lax.axis_index("row")
    frames, rows = lax.axis_size("frame"), lax.axis_size("row")
    tiles = [(kv, 0), (kv_a, 0), (kv_b, 0)]
    tiles += [(kv_fa, 0), (corner_fa, 0), (corner_fa, 2 * TILE)]
    tiles += [(kv_fb, 0), (corner_fb, 0), (corner_fb, 2 * TILE)]
    gather_near(tiles, key_ref, value_ref)
    lane = lax.broadcasted_iota(jnp.int32, (1, WIDE), 1)
    bias = jnp.zeros((1, WIDE), jnp.float32)
    for slot, (a, b) in enumerate(slot_offsets()):
        bit = pairs_s[0, 0, 0, 9 * (a + 1) + 3 * (b + 1) + 1]
        inside = (frame + a >= 0) & (frame + a < frames) & (row + b >= 0) & (row + b < rows)
        level = jnp.where((bit == 1) & inside, 0.0, -FAR).astype(jnp.float32)
        here = (lane >= slot * TILE) & (lane < (slot + 1) * TILE)
        bias = jnp.where(here, level, bias)
    stat_lane = lax.broadcasted_iota(jnp.int32, (TILE, 128), 1)
    stats = jnp.zeros((TILE, 128), jnp.float32)
    count = own_qg.shape[1] // HEAD_DIM
    for h in range(count):
        feat = slice(h * HEAD_DIM, (h + 1) * HEAD_DIM)
        query, grad = own_qg[0:TILE, feat], own_qg[TILE : 2 * TILE, feat]
        scores = lax.dot_general(
            query, key_ref[:, feat], (((1,), (1,)), ((), ())), preferred_element_type=jnp.float32
        )
        scores = scores * SCALE2 + bias
        top = jnp.max(scores, axis=1, keepdims=True)
        weights = jnp.exp2(scores - top)
        total = jnp.sum(weights, axis=1, keepdims=True)
        rounded = (weights * (1.0 / total)).astype(jnp.bfloat16)
        attended = jnp.dot(rounded, value_ref[:, feat], preferred_element_type=jnp.float32)
        attended = attended.astype(jnp.bfloat16)
        spread = jnp.sum(
            grad.astype(jnp.float32) * attended.astype(jnp.float32), axis=1, keepdims=True
        )
        attended_ref[:, feat] = attended
        stats = jnp.where(stat_lane == h, top + jnp.log2(total), stats)
        stats = jnp.where(stat_lane == count + h, spread, stats)
    bias_ref[...] = bias
    column_ref[...] = stats
    stat_ref[...] = stats.T[0:8, :]
    stat_ref[7:8, 0:27] = pairs_v[0, 0].astype(jnp.float32)


def query_grad_kernel(heads, own_qg, key_ref, value_ref, attended_ref, column_ref, bias_ref, *refs):
    far_ref, near_ref = refs
    bias = bias_ref[...]
    count = own_qg.shape[1] // HEAD_DIM
    grad_parts = []
    for h in range(count):
        feat = slice(h * HEAD_DIM, (h + 1) * HEAD_DIM)
        query, grad = own_qg[0:TILE, feat], own_qg[TILE : 2 * TILE, feat]
        key = key_ref[:, feat]
        scores = lax.dot_general(
            query, key, (((1,), (1,)), ((), ())), preferred_element_type=jnp.float32
        )
        weights = jnp.exp2(scores * SCALE2 + bias - column_ref[:, h : h + 1])
        pushes = lax.dot_general(
            grad, value_ref[:, feat], (((1,), (1,)), ((), ())), preferred_element_type=jnp.float32
        )
        spread = column_ref[:, count + h : count + h + 1]
        slopes = (weights * (pushes - spread)).astype(jnp.bfloat16)
        query_grad = SCALE * jnp.dot(slopes, key, preferred_element_type=jnp.float32)
        grad_parts.append(query_grad.astype(jnp.bfloat16))
    blocks = column_blocks([attended_ref[...]], grad_parts, heads)
    for i in range(2):
        far_ref[i] = blocks[heads // 2][i]
        for at, k in enumerate(near_heads(heads)):
            near_ref[at, i] = blocks[k][i]


def key_kernel(sides, *refs):
    kvs, refs = refs[: len(sides)], refs[len(sides) :]
    (qg, qg_a, qg_b, st, st_a, st_b), refs = refs[:6], refs[6:]
    outs, (query_ref, grad_ref, stat_ref) = refs[: len(sides)], refs[len(sides) :]
    count = qg.shape[1] // HEAD_DIM
    frame, frames = lax.axis_index("frame"), lax.axis_size("frame")
    gather_near([(qg, 0), (qg_a, 0), (qg_b, 0)], query_ref, grad_ref)
    lane = lax.broadcasted_iota(jnp.int32, (1, TILE), 1)
    level = lax.broadcasted_iota(jnp.int32, (8, TILE), 0)
    frame_steps = [slot_steps("frame")[side] for side in sides]
    for slot, (ref, b) in enumerate(zip((st, st_a, st_b), slot_steps("row"))):
        block = ref[...]
        for i, a in enumerate(frame_steps):
            index = 9 * (a + 1) + 3 * (1 - b) + 1
            bit = jnp.sum(jnp.where(lane == index, block[7:8, :], 0.0), axis=1, keepdims=True)
            inside = (frame + a >= 0) & (frame + a < frames)
            bit = bit * jnp.where(inside, 1.0, 0.0).astype(jnp.float32)
            closed = (level < count) & (bit < 0.5)
            stat_ref[i, :, slot * TILE : (slot + 1) * TILE] = jnp.where(closed, FAR, block)
    for h in range(count):
        feat = slice(h * HEAD_DIM, (h + 1) * HEAD_DIM)
        query, grad = query_ref[:, feat], grad_ref[:, feat]
        for i, (kv_ref, out_ref) in enumerate(zip(kvs, outs)):
            key, value = kv_ref[0:TILE, feat], kv_ref[TILE : 2 * TILE, feat]
            scores = lax.dot_general(
                key, query, (((1,), (1,)), ((), ())), preferred_element_type=jnp.float32
            )
            weights = jnp.exp2(scores * SCALE2 - stat_ref[i, h : h + 1, :])
            rounded = weights.astype(jnp.bfloat16)
            value_grad = jnp.dot(rounded, grad, preferred_element_type=jnp.float32)
            pushes = lax.dot_general(
                value, grad, (((1,), (1,)), ((), ())), preferred_element_type=jnp.float32
            )
            spread = stat_ref[i, count + h : count + h + 1, :]
            slopes = (weights * (pushes - spread)).astype(jnp.bfloat16)
            key_grad = SCALE * jnp.dot(slopes, query, preferred_element_type=jnp.float32)
            out_ref[0:TILE, feat] = key_grad.astype(out_ref.dtype)
            out_ref[TILE : 2 * TILE, feat] = value_grad.astype(out_ref.dtype)


def fold_kernel(heads, own_ref, got_a, got_b, near_q, far_ref, *near_refs):
    total = own_ref[...] + got_a[...].astype(jnp.float32) + got_b[...].astype(jnp.float32)
    total = total.astype(jnp.bfloat16)
    blocks = column_blocks([total[0:TILE]], [total[TILE : 2 * TILE]], heads)
    for i in range(2):
        far_ref[i] = blocks[heads // 2][i]
        for at, (k, ref) in enumerate(zip(near_heads(heads), near_refs)):
            ref[i] = near_q[at, i]
            ref[2 + i] = blocks[k][i]


def after(value, *others):
    return lax.optimization_barrier((value,) + others)[0]


def head_swap(value, k):
    count = lax.axis_size("head")
    return lax.ppermute(value, "head", [(i, i ^ k) for i in range(count)]) if k else value


def stacked(first, second):
    rows = first.shape[0]
    low = jnp.pad(first, ((0, rows), (0, 0)), constant_values=-jnp.inf)
    return jnp.maximum(low, jnp.pad(second, ((rows, 0), (0, 0)), constant_values=-jnp.inf))


def body(queries, key_tokens, value_tokens, grad_out, tile_pairs):
    frames_dev, rows_dev, columns, feats = queries.shape
    heads = lax.axis_size("head")
    bf16, f32 = jnp.bfloat16, jnp.float32
    flat = [x.reshape(TILE, feats) for x in (key_tokens, value_tokens, queries, grad_out)]

    kv = stacked(flat[0], flat[1])
    qg = stacked(flat[2], flat[3])
    kv_a, kv_b = pair_swap(kv, "row", 0), pair_swap(kv, "row", 1)
    kv_fb, kv_fa = pair_swap(kv, "frame", 1), pair_swap(kv, "frame", 0)
    rows = call(regroup_kernel, jax.ShapeDtypeStruct((4 * TILE, feats), bf16), [VMEM] * 2, VMEM)(
        kv_a, kv_b
    )
    rows = after(rows, kv_fb, kv_fa)
    corner_fb, corner_fa = pair_swap(rows, "frame", 1), pair_swap(rows, "frame", 0)
    qg_late = after(qg, kv_fb, kv_fa)
    qg_a, qg_b = pair_swap(qg_late, "row", 0), pair_swap(qg_late, "row", 1)

    span = TILE // heads
    pair, four = (jax.ShapeDtypeStruct((n, span, feats), bf16) for n in (2, 4))
    near_shape = jax.ShapeDtypeStruct((heads - 1, 2, span, feats), bf16)
    wide = jax.ShapeDtypeStruct((WIDE, feats), bf16)
    attended, stat, column, bias, key_near, value_near = call(
        query_kernel,
        (
            jax.ShapeDtypeStruct((TILE, feats), bf16),
            jax.ShapeDtypeStruct((8, TILE), f32),
            jax.ShapeDtypeStruct((TILE, 128), f32),
            jax.ShapeDtypeStruct((1, WIDE), f32),
            wide,
            wide,
        ),
        [SMEM] + [VMEM] * 9,
        (VMEM,) * 6,
    )(tile_pairs, tile_pairs, qg, kv, kv_a, kv_b, kv_fb, kv_fa, corner_fb, corner_fa)
    st_a, st_b = pair_swap(stat, "row", 0), pair_swap(stat, "row", 1)

    def terms(sides, kinds, *kvs):
        row_near = pltpu.VMEM((3 * TILE, feats), bf16)
        return call(
            lambda *refs: key_kernel(sides, *refs),
            [jax.ShapeDtypeStruct((2 * TILE, feats), kind) for kind in kinds],
            [VMEM] * (len(sides) + 6),
            [VMEM] * len(sides),
            [row_near, row_near, pltpu.VMEM((len(sides), 8, 3 * TILE), f32)],
        )(*kvs, qg, qg_a, qg_b, stat, st_a, st_b)

    term_b, term_a = terms((2, 1), (bf16, bf16), kv_fb, kv_fa)
    got_b, got_a = pair_swap(term_b, "frame", 1), pair_swap(term_a, "frame", 0)
    (own,) = terms((0,), (f32,), after(kv, got_a))
    far_q, near_q = call(
        lambda *refs: query_grad_kernel(heads, *refs),
        (pair, near_shape),
        [VMEM] * 6,
        (VMEM, VMEM),
    )(after(qg, got_a), key_near, value_near, attended, column, bias)
    got_far_q = head_swap(far_q, heads // 2)

    far_k, *near_k = call(
        lambda *refs: fold_kernel(heads, *refs),
        [pair] + [four] * (heads - 1),
        [VMEM] * 4,
        [VMEM] * heads,
    )(own, got_b, got_a, near_q)
    got_far_k = head_swap(after(far_k, got_far_q), heads // 2)
    got_near = [head_swap(sent, k) for k, sent in zip(near_heads(heads), near_k)]

    out = jax.ShapeDtypeStruct((frames_dev * rows_dev, columns // heads, heads * feats), bf16)
    outs = call(
        lambda *refs: assemble_kernel(heads, *refs),
        [out] * 4,
        [VMEM] * (heads + 1),
        [VMEM] * 4,
    )(got_far_q, got_far_k, *got_near)
    return tuple(x.reshape((frames_dev, rows_dev) + out.shape[1:]) for x in outs)


def solution(mesh):
    inputs = P("frame", "row", None, "head")
    outputs = P("frame", "row", "head", None)
    return jax.shard_map(
        body,
        mesh=mesh,
        in_specs=(inputs,) * 4 + (P("frame", "row", None, None),),
        out_specs=(outputs,) * 4,
        check_vma=False,
    )
```

```python
import jax
import jax.numpy as jnp
from jax import lax
from jax.experimental import pallas as pl
from jax.experimental.pallas import tpu as pltpu
from jax.sharding import PartitionSpec as P

HEAD_DIM = 128
TILE = 192
SLOTS = 9
WIDE = SLOTS * TILE
SCALE = HEAD_DIM**-0.5
SCALE2 = SCALE * 1.4426950408889634
FAR = 1e30
VMEM_LIMIT = 48 * 1024 * 1024

VMEM = pl.BlockSpec(memory_space=pltpu.VMEM)
SMEM = pl.BlockSpec(memory_space=pltpu.SMEM)


def call(kernel, outs, in_specs, out_specs, scratch=()):
    return pl.pallas_call(
        kernel,
        out_shape=outs,
        in_specs=in_specs,
        out_specs=out_specs,
        scratch_shapes=list(scratch),
        compiler_params=pltpu.CompilerParams(vmem_limit_bytes=VMEM_LIMIT),
    )


def pair_swap(value, axis, parity):
    count = lax.axis_size(axis)
    pairs = []
    for low in range(parity, count - 1, 2):
        pairs += [(low, low + 1), (low + 1, low)]
    return lax.ppermute(value, axis, pairs)


def slot_steps(axis):
    near = 1 - 2 * (lax.axis_index(axis) % 2)
    return (0, near, -near)


def slot_offsets():
    return [(a, b) for a in slot_steps("frame") for b in slot_steps("row")]


def regroup_kernel(a_ref, b_ref, out_ref):
    out_ref[0 : 2 * TILE, :] = a_ref[...]
    out_ref[2 * TILE : 4 * TILE, :] = b_ref[...]


def gather_near(tiles, first_ref, second_ref):
    for slot, (ref, start) in enumerate(tiles):
        rows = slice(slot * TILE, (slot + 1) * TILE)
        first_ref[rows, :] = ref[start : start + TILE, :]
        second_ref[rows, :] = ref[start + TILE : start + 2 * TILE, :]


def store_sends(send_ref, firsts, seconds):
    heads = send_ref.shape[0]
    group, span = 8 // heads, TILE // heads
    row = lax.broadcasted_iota(jnp.int32, (TILE, TILE), 0)
    col = lax.broadcasted_iota(jnp.int32, (TILE, TILE), 1)
    block = jnp.zeros_like(row)
    for d in range(1, heads):
        block += (row >= d * span).astype(jnp.int32)
    inner = row - block * span
    shift = group.bit_length() - 1
    source = (inner >> shift) * 8 + block * group + (inner & (group - 1))
    order = (col == source).astype(jnp.bfloat16)
    joined = jnp.concatenate(firsts + seconds, axis=1)
    moved = jnp.dot(order, joined, preferred_element_type=jnp.float32).astype(jnp.bfloat16)
    feats = send_ref.shape[3]
    for k in range(heads):
        rows = slice(k * span, (k + 1) * span)
        send_ref[k, 0] = moved[rows, :feats]
        send_ref[k, 1] = moved[rows, feats:]


def assemble(got_ref, out_refs):
    heads, _, _, feats = got_ref.shape
    for k in range(heads):
        place = slice(k * feats, (k + 1) * feats)
        for i, out_ref in enumerate(out_refs):
            out_ref[:, :, place] = got_ref[k, i].reshape(out_ref.shape[:2] + (feats,))


def assemble_kernel(got_ref, *out_refs):
    assemble(got_ref, out_refs)


def query_kernel(
    pairs_s, pairs_v, own_qg, kv, kv_a, kv_b, kv_fb, kv_fa, corner_fb, corner_fa, *refs
):
    attended_ref, stat_ref, column_ref, bias_ref, key_ref, value_ref = refs
    frame, row = lax.axis_index("frame"), lax.axis_index("row")
    frames, rows = lax.axis_size("frame"), lax.axis_size("row")
    tiles = [(kv, 0), (kv_a, 0), (kv_b, 0)]
    tiles += [(kv_fa, 0), (corner_fa, 0), (corner_fa, 2 * TILE)]
    tiles += [(kv_fb, 0), (corner_fb, 0), (corner_fb, 2 * TILE)]
    gather_near(tiles, key_ref, value_ref)
    lane = lax.broadcasted_iota(jnp.int32, (1, WIDE), 1)
    bias = jnp.zeros((1, WIDE), jnp.float32)
    for slot, (a, b) in enumerate(slot_offsets()):
        bit = pairs_s[0, 0, 0, 9 * (a + 1) + 3 * (b + 1) + 1]
        inside = (frame + a >= 0) & (frame + a < frames) & (row + b >= 0) & (row + b < rows)
        level = jnp.where((bit == 1) & inside, 0.0, -FAR).astype(jnp.float32)
        here = (lane >= slot * TILE) & (lane < (slot + 1) * TILE)
        bias = jnp.where(here, level, bias)
    stat_lane = lax.broadcasted_iota(jnp.int32, (TILE, 128), 1)
    stats = jnp.zeros((TILE, 128), jnp.float32)
    count = own_qg.shape[1] // HEAD_DIM
    for h in range(count):
        feat = slice(h * HEAD_DIM, (h + 1) * HEAD_DIM)
        query, grad = own_qg[0:TILE, feat], own_qg[TILE : 2 * TILE, feat]
        scores = lax.dot_general(
            query, key_ref[:, feat], (((1,), (1,)), ((), ())), preferred_element_type=jnp.float32
        )
        scores = scores * SCALE2 + bias
        top = jnp.max(scores, axis=1, keepdims=True)
        weights = jnp.exp2(scores - top)
        total = jnp.sum(weights, axis=1, keepdims=True)
        rounded = (weights * (1.0 / total)).astype(jnp.bfloat16)
        attended = jnp.dot(rounded, value_ref[:, feat], preferred_element_type=jnp.float32)
        attended = attended.astype(jnp.bfloat16)
        spread = jnp.sum(
            grad.astype(jnp.float32) * attended.astype(jnp.float32), axis=1, keepdims=True
        )
        attended_ref[:, feat] = attended
        stats = jnp.where(stat_lane == h, top + jnp.log2(total), stats)
        stats = jnp.where(stat_lane == count + h, spread, stats)
    bias_ref[...] = bias
    column_ref[...] = stats
    stat_ref[...] = stats.T[0:8, :]
    stat_ref[7:8, 0:27] = pairs_v[0, 0].astype(jnp.float32)


def query_grad_kernel(own_qg, key_ref, value_ref, attended_ref, column_ref, bias_ref, send_ref):
    bias = bias_ref[...]
    count = own_qg.shape[1] // HEAD_DIM
    grad_parts = []
    for h in range(count):
        feat = slice(h * HEAD_DIM, (h + 1) * HEAD_DIM)
        query, grad = own_qg[0:TILE, feat], own_qg[TILE : 2 * TILE, feat]
        key = key_ref[:, feat]
        scores = lax.dot_general(
            query, key, (((1,), (1,)), ((), ())), preferred_element_type=jnp.float32
        )
        weights = jnp.exp2(scores * SCALE2 + bias - column_ref[:, h : h + 1])
        pushes = lax.dot_general(
            grad, value_ref[:, feat], (((1,), (1,)), ((), ())), preferred_element_type=jnp.float32
        )
        spread = column_ref[:, count + h : count + h + 1]
        slopes = (weights * (pushes - spread)).astype(jnp.bfloat16)
        query_grad = SCALE * jnp.dot(slopes, key, preferred_element_type=jnp.float32)
        grad_parts.append(query_grad.astype(jnp.bfloat16))
    store_sends(send_ref, [attended_ref[...]], grad_parts)


def key_kernel(sides, *refs):
    kvs, refs = refs[: len(sides)], refs[len(sides) :]
    (qg, qg_a, qg_b, st, st_a, st_b), refs = refs[:6], refs[6:]
    outs, (query_ref, grad_ref, stat_ref) = refs[: len(sides)], refs[len(sides) :]
    count = qg.shape[1] // HEAD_DIM
    frame, frames = lax.axis_index("frame"), lax.axis_size("frame")
    gather_near([(qg, 0), (qg_a, 0), (qg_b, 0)], query_ref, grad_ref)
    lane = lax.broadcasted_iota(jnp.int32, (1, TILE), 1)
    level = lax.broadcasted_iota(jnp.int32, (8, TILE), 0)
    frame_steps = [slot_steps("frame")[side] for side in sides]
    for slot, (ref, b) in enumerate(zip((st, st_a, st_b), slot_steps("row"))):
        block = ref[...]
        for i, a in enumerate(frame_steps):
            index = 9 * (a + 1) + 3 * (1 - b) + 1
            bit = jnp.sum(jnp.where(lane == index, block[7:8, :], 0.0), axis=1, keepdims=True)
            inside = (frame + a >= 0) & (frame + a < frames)
            bit = bit * jnp.where(inside, 1.0, 0.0).astype(jnp.float32)
            closed = (level < count) & (bit < 0.5)
            stat_ref[i, :, slot * TILE : (slot + 1) * TILE] = jnp.where(closed, FAR, block)
    for h in range(count):
        feat = slice(h * HEAD_DIM, (h + 1) * HEAD_DIM)
        query, grad = query_ref[:, feat], grad_ref[:, feat]
        keys = jnp.concatenate([ref[0:TILE, feat] for ref in kvs], axis=0)
        values = jnp.concatenate([ref[TILE : 2 * TILE, feat] for ref in kvs], axis=0)
        scores = lax.dot_general(
            keys, query, (((1,), (1,)), ((), ())), preferred_element_type=jnp.float32
        )
        pushes = lax.dot_general(
            values, grad, (((1,), (1,)), ((), ())), preferred_element_type=jnp.float32
        )
        rounded, slopes = [], []
        for i in range(len(sides)):
            rows = slice(i * TILE, (i + 1) * TILE)
            weights = jnp.exp2(scores[rows] * SCALE2 - stat_ref[i, h : h + 1, :])
            spread = stat_ref[i, count + h : count + h + 1, :]
            rounded.append(weights.astype(jnp.bfloat16))
            slopes.append((weights * (pushes[rows] - spread)).astype(jnp.bfloat16))
        rounded, slopes = jnp.concatenate(rounded, axis=0), jnp.concatenate(slopes, axis=0)
        value_grad = jnp.dot(rounded, grad, preferred_element_type=jnp.float32)
        key_grad = SCALE * jnp.dot(slopes, query, preferred_element_type=jnp.float32)
        for i, ref in enumerate(outs):
            rows = slice(i * TILE, (i + 1) * TILE)
            ref[0:TILE, feat] = key_grad[rows].astype(ref.dtype)
            ref[TILE : 2 * TILE, feat] = value_grad[rows].astype(ref.dtype)


def fold_kernel(own_ref, got_a, got_b, send_ref):
    total = own_ref[...] + got_a[...].astype(jnp.float32) + got_b[...].astype(jnp.float32)
    total = total.astype(jnp.bfloat16)
    store_sends(send_ref, [total[0:TILE]], [total[TILE : 2 * TILE]])


def after(value, *others):
    return lax.optimization_barrier((value,) + others)[0]


def stacked(first, second):
    rows = first.shape[0]
    low = jnp.pad(first, ((0, rows), (0, 0)), constant_values=-jnp.inf)
    return jnp.maximum(low, jnp.pad(second, ((rows, 0), (0, 0)), constant_values=-jnp.inf))


def body(queries, key_tokens, value_tokens, grad_out, tile_pairs):
    frames_dev, rows_dev, columns, feats = queries.shape
    heads = lax.axis_size("head")
    bf16, f32 = jnp.bfloat16, jnp.float32
    flat = [x.reshape(TILE, feats) for x in (key_tokens, value_tokens, queries, grad_out)]

    kv = stacked(flat[0], flat[1])
    qg = stacked(flat[2], flat[3])
    kv_a, kv_b = pair_swap(kv, "row", 0), pair_swap(kv, "row", 1)
    kv_fb, kv_fa = pair_swap(kv, "frame", 1), pair_swap(kv, "frame", 0)
    rows = call(regroup_kernel, jax.ShapeDtypeStruct((4 * TILE, feats), bf16), [VMEM] * 2, VMEM)(
        kv_a, kv_b
    )
    rows = after(rows, kv_fb, kv_fa)
    corner_fb, corner_fa = pair_swap(rows, "frame", 1), pair_swap(rows, "frame", 0)
    qg_late = after(qg, kv_fb, kv_fa)
    qg_a, qg_b = pair_swap(qg_late, "row", 0), pair_swap(qg_late, "row", 1)

    send_shape = jax.ShapeDtypeStruct((heads, 2, TILE // heads, feats), bf16)
    wide = jax.ShapeDtypeStruct((WIDE, feats), bf16)
    attended, stat, column, bias, key_near, value_near = call(
        query_kernel,
        (
            jax.ShapeDtypeStruct((TILE, feats), bf16),
            jax.ShapeDtypeStruct((8, TILE), f32),
            jax.ShapeDtypeStruct((TILE, 128), f32),
            jax.ShapeDtypeStruct((1, WIDE), f32),
            wide,
            wide,
        ),
        [SMEM] + [VMEM] * 9,
        (VMEM,) * 6,
    )(tile_pairs, tile_pairs, qg, kv, kv_a, kv_b, kv_fb, kv_fa, corner_fb, corner_fa)
    st_a, st_b = pair_swap(stat, "row", 0), pair_swap(stat, "row", 1)

    def terms(sides, kinds, *kvs):
        row_near = pltpu.VMEM((3 * TILE, feats), bf16)
        return call(
            lambda *refs: key_kernel(sides, *refs),
            [jax.ShapeDtypeStruct((2 * TILE, feats), kind) for kind in kinds],
            [VMEM] * (len(sides) + 6),
            [VMEM] * len(sides),
            [row_near, row_near, pltpu.VMEM((len(sides), 8, 3 * TILE), f32)],
        )(*kvs, qg, qg_a, qg_b, stat, st_a, st_b)

    term_b, term_a = terms((2, 1), (bf16, bf16), kv_fb, kv_fa)
    got_b, got_a = pair_swap(term_b, "frame", 1), pair_swap(term_a, "frame", 0)
    (own,) = terms((0,), (f32,), after(kv, got_a))
    sent_q = call(query_grad_kernel, send_shape, [VMEM] * 6, VMEM)(
        after(qg, got_a), key_near, value_near, attended, column, bias
    )
    sent_k = call(fold_kernel, send_shape, [VMEM] * 3, VMEM)(after(own, sent_q), got_b, got_a)

    out = jax.ShapeDtypeStruct((frames_dev * rows_dev, columns // heads, heads * feats), bf16)
    outs = []
    for sent in (sent_q, sent_k):
        got = lax.all_to_all(sent, "head", split_axis=0, concat_axis=0, tiled=True)
        outs += call(assemble_kernel, (out, out), [VMEM], (VMEM, VMEM))(got)
    return tuple(x.reshape((frames_dev, rows_dev) + out.shape[1:]) for x in outs)


def solution(mesh):
    inputs = P("frame", "row", None, "head")
    outputs = P("frame", "row", "head", None)
    return jax.shard_map(
        body,
        mesh=mesh,
        in_specs=(inputs,) * 4 + (P("frame", "row", None, None),),
        out_specs=(outputs,) * 4,
        check_vma=False,
    )
```

```python
import jax
import jax.numpy as jnp
from jax import lax
from jax.experimental import pallas as pl
from jax.experimental.pallas import tpu as pltpu
from jax.sharding import PartitionSpec as P

HEAD_DIM = 128
TILE = 192
SLOTS = 9
WIDE = SLOTS * TILE
SCALE = HEAD_DIM**-0.5
SCALE2 = SCALE * 1.4426950408889634
FAR = 1e30
VMEM_LIMIT = 48 * 1024 * 1024

VMEM = pl.BlockSpec(memory_space=pltpu.VMEM)
SMEM = pl.BlockSpec(memory_space=pltpu.SMEM)


def call(kernel, outs, in_specs, out_specs, scratch=()):
    return pl.pallas_call(
        kernel,
        out_shape=outs,
        in_specs=in_specs,
        out_specs=out_specs,
        scratch_shapes=list(scratch),
        compiler_params=pltpu.CompilerParams(vmem_limit_bytes=VMEM_LIMIT),
    )


def pair_swap(value, axis, parity):
    count = lax.axis_size(axis)
    pairs = []
    for low in range(parity, count - 1, 2):
        pairs += [(low, low + 1), (low + 1, low)]
    return lax.ppermute(value, axis, pairs)


def slot_steps(axis):
    near = 1 - 2 * (lax.axis_index(axis) % 2)
    return (0, near, -near)


def slot_offsets():
    return [(a, b) for a in slot_steps("frame") for b in slot_steps("row")]


def regroup_kernel(own_ref, a_ref, b_ref, out_ref):
    for i, ref in enumerate((own_ref, a_ref, b_ref)):
        out_ref[2 * TILE * i : 2 * TILE * (i + 1), :] = ref[...]


def gather_near(tiles, first_ref, second_ref):
    for slot, (ref, start) in enumerate(tiles):
        rows = slice(slot * TILE, (slot + 1) * TILE)
        first_ref[rows, :] = ref[start : start + TILE, :]
        second_ref[rows, :] = ref[start + TILE : start + 2 * TILE, :]


def column_blocks(firsts, seconds, heads):
    group, span = 8 // heads, TILE // heads
    me = lax.axis_index("head")
    row = lax.broadcasted_iota(jnp.int32, (TILE, TILE), 0)
    col = lax.broadcasted_iota(jnp.int32, (TILE, TILE), 1)
    block = jnp.zeros_like(row)
    for d in range(1, heads):
        block += (row >= d * span).astype(jnp.int32)
    inner = row - block * span
    shift = group.bit_length() - 1
    source = (inner >> shift) * 8 + (block ^ me) * group + (inner & (group - 1))
    order = (col == source).astype(jnp.bfloat16)
    joined = jnp.concatenate(firsts + seconds, axis=1)
    moved = jnp.dot(order, joined, preferred_element_type=jnp.float32).astype(jnp.bfloat16)
    feats = joined.shape[1] // 2
    return [
        [moved[k * span : (k + 1) * span, i * feats : (i + 1) * feats] for i in range(2)]
        for k in range(heads)
    ]


def near_heads(heads):
    return [k for k in range(heads) if k != heads // 2]


def assemble_kernel(heads, far_q, far_k, *refs):
    near_refs, out_refs = refs[: heads - 1], refs[heads - 1 :]
    feats = far_q.shape[2]
    me = lax.axis_index("head")

    def put(k, i, rows):
        place = pl.ds(pl.multiple_of((me ^ k) * feats, HEAD_DIM), feats)
        out_refs[i][:, :, place] = rows.reshape(out_refs[i].shape[:2] + (feats,))

    for i in range(2):
        put(heads // 2, i, far_q[i])
        put(heads // 2, 2 + i, far_k[i])
    for k, ref in zip(near_heads(heads), near_refs):
        for i in range(4):
            put(k, i, ref[i])


def query_kernel(pairs_s, pairs_v, own_qg, kv, kv_fb, kv_fa, *refs):
    attended_ref, stat_ref, column_ref, bias_ref, key_ref, value_ref = refs
    frame, row = lax.axis_index("frame"), lax.axis_index("row")
    frames, rows = lax.axis_size("frame"), lax.axis_size("row")
    tiles = [(ref, 2 * TILE * i) for ref in (kv, kv_fa, kv_fb) for i in range(3)]
    gather_near(tiles, key_ref, value_ref)
    lane = lax.broadcasted_iota(jnp.int32, (1, WIDE), 1)
    bias = jnp.zeros((1, WIDE), jnp.float32)
    for slot, (a, b) in enumerate(slot_offsets()):
        bit = pairs_s[0, 0, 0, 9 * (a + 1) + 3 * (b + 1) + 1]
        inside = (frame + a >= 0) & (frame + a < frames) & (row + b >= 0) & (row + b < rows)
        level = jnp.where((bit == 1) & inside, 0.0, -FAR).astype(jnp.float32)
        here = (lane >= slot * TILE) & (lane < (slot + 1) * TILE)
        bias = jnp.where(here, level, bias)
    stat_lane = lax.broadcasted_iota(jnp.int32, (TILE, 128), 1)
    stats = jnp.zeros((TILE, 128), jnp.float32)
    count = own_qg.shape[1] // HEAD_DIM
    for h in range(count):
        feat = slice(h * HEAD_DIM, (h + 1) * HEAD_DIM)
        query, grad = own_qg[0:TILE, feat], own_qg[TILE : 2 * TILE, feat]
        scores = lax.dot_general(
            query, key_ref[:, feat], (((1,), (1,)), ((), ())), preferred_element_type=jnp.float32
        )
        scores = scores * SCALE2 + bias
        top = jnp.max(scores, axis=1, keepdims=True)
        weights = jnp.exp2(scores - top)
        total = jnp.sum(weights, axis=1, keepdims=True)
        rounded = (weights * (1.0 / total)).astype(jnp.bfloat16)
        attended = jnp.dot(rounded, value_ref[:, feat], preferred_element_type=jnp.float32)
        attended = attended.astype(jnp.bfloat16)
        spread = jnp.sum(
            grad.astype(jnp.float32) * attended.astype(jnp.float32), axis=1, keepdims=True
        )
        attended_ref[:, feat] = attended
        stats = jnp.where(stat_lane == h, top + jnp.log2(total), stats)
        stats = jnp.where(stat_lane == count + h, spread, stats)
    bias_ref[...] = bias
    column_ref[...] = stats
    stat_ref[...] = stats.T[0:8, :]
    stat_ref[7:8, 0:27] = pairs_v[0, 0].astype(jnp.float32)


def query_grad_kernel(heads, own_qg, key_ref, value_ref, attended_ref, column_ref, bias_ref, *refs):
    far_ref, near_ref = refs
    bias = bias_ref[...]
    count = own_qg.shape[1] // HEAD_DIM
    grad_parts = []
    for h in range(count):
        feat = slice(h * HEAD_DIM, (h + 1) * HEAD_DIM)
        query, grad = own_qg[0:TILE, feat], own_qg[TILE : 2 * TILE, feat]
        key = key_ref[:, feat]
        scores = lax.dot_general(
            query, key, (((1,), (1,)), ((), ())), preferred_element_type=jnp.float32
        )
        weights = jnp.exp2(scores * SCALE2 + bias - column_ref[:, h : h + 1])
        pushes = lax.dot_general(
            grad, value_ref[:, feat], (((1,), (1,)), ((), ())), preferred_element_type=jnp.float32
        )
        spread = column_ref[:, count + h : count + h + 1]
        slopes = (weights * (pushes - spread)).astype(jnp.bfloat16)
        query_grad = SCALE * jnp.dot(slopes, key, preferred_element_type=jnp.float32)
        grad_parts.append(query_grad.astype(jnp.bfloat16))
    blocks = column_blocks([attended_ref[...]], grad_parts, heads)
    for i in range(2):
        far_ref[i] = blocks[heads // 2][i]
        for at, k in enumerate(near_heads(heads)):
            near_ref[at, i] = blocks[k][i]


def key_kernel(sides, *refs):
    kvs, refs = refs[: len(sides)], refs[len(sides) :]
    (qg, qg_a, qg_b, st, st_a, st_b), refs = refs[:6], refs[6:]
    outs, (query_ref, grad_ref, stat_ref) = refs[: len(sides)], refs[len(sides) :]
    count = qg.shape[1] // HEAD_DIM
    frame, frames = lax.axis_index("frame"), lax.axis_size("frame")
    gather_near([(qg, 0), (qg_a, 0), (qg_b, 0)], query_ref, grad_ref)
    lane = lax.broadcasted_iota(jnp.int32, (1, TILE), 1)
    level = lax.broadcasted_iota(jnp.int32, (8, TILE), 0)
    frame_steps = [slot_steps("frame")[side] for side in sides]
    for slot, (ref, b) in enumerate(zip((st, st_a, st_b), slot_steps("row"))):
        block = ref[...]
        for i, a in enumerate(frame_steps):
            index = 9 * (a + 1) + 3 * (1 - b) + 1
            bit = jnp.sum(jnp.where(lane == index, block[7:8, :], 0.0), axis=1, keepdims=True)
            inside = (frame + a >= 0) & (frame + a < frames)
            bit = bit * jnp.where(inside, 1.0, 0.0).astype(jnp.float32)
            closed = (level < count) & (bit < 0.5)
            stat_ref[i, :, slot * TILE : (slot + 1) * TILE] = jnp.where(closed, FAR, block)
    for h in range(count):
        feat = slice(h * HEAD_DIM, (h + 1) * HEAD_DIM)
        query, grad = query_ref[:, feat], grad_ref[:, feat]
        keys = jnp.concatenate([ref[0:TILE, feat] for ref in kvs], axis=0)
        values = jnp.concatenate([ref[TILE : 2 * TILE, feat] for ref in kvs], axis=0)
        scores = lax.dot_general(
            keys, query, (((1,), (1,)), ((), ())), preferred_element_type=jnp.float32
        )
        pushes = lax.dot_general(
            values, grad, (((1,), (1,)), ((), ())), preferred_element_type=jnp.float32
        )
        rounded, slopes = [], []
        for i in range(len(sides)):
            rows = slice(i * TILE, (i + 1) * TILE)
            weights = jnp.exp2(scores[rows] * SCALE2 - stat_ref[i, h : h + 1, :])
            spread = stat_ref[i, count + h : count + h + 1, :]
            rounded.append(weights.astype(jnp.bfloat16))
            slopes.append((weights * (pushes[rows] - spread)).astype(jnp.bfloat16))
        rounded, slopes = jnp.concatenate(rounded, axis=0), jnp.concatenate(slopes, axis=0)
        value_grad = jnp.dot(rounded, grad, preferred_element_type=jnp.float32)
        key_grad = SCALE * jnp.dot(slopes, query, preferred_element_type=jnp.float32)
        for i, ref in enumerate(outs):
            rows = slice(i * TILE, (i + 1) * TILE)
            ref[0:TILE, feat] = key_grad[rows].astype(ref.dtype)
            ref[TILE : 2 * TILE, feat] = value_grad[rows].astype(ref.dtype)


def fold_kernel(heads, own_ref, got_a, got_b, near_q, far_ref, *near_refs):
    total = own_ref[...] + got_a[...].astype(jnp.float32) + got_b[...].astype(jnp.float32)
    total = total.astype(jnp.bfloat16)
    blocks = column_blocks([total[0:TILE]], [total[TILE : 2 * TILE]], heads)
    for i in range(2):
        far_ref[i] = blocks[heads // 2][i]
        for at, (k, ref) in enumerate(zip(near_heads(heads), near_refs)):
            ref[i] = near_q[at, i]
            ref[2 + i] = blocks[k][i]


def after(value, *others):
    return lax.optimization_barrier((value,) + others)[0]


def head_swap(value, k):
    count = lax.axis_size("head")
    return lax.ppermute(value, "head", [(i, i ^ k) for i in range(count)]) if k else value


def stacked(first, second):
    rows = first.shape[0]
    low = jnp.pad(first, ((0, rows), (0, 0)), constant_values=-jnp.inf)
    return jnp.maximum(low, jnp.pad(second, ((rows, 0), (0, 0)), constant_values=-jnp.inf))


def body(queries, key_tokens, value_tokens, grad_out, tile_pairs):
    frames_dev, rows_dev, columns, feats = queries.shape
    heads = lax.axis_size("head")
    bf16, f32 = jnp.bfloat16, jnp.float32
    flat = [x.reshape(TILE, feats) for x in (key_tokens, value_tokens, queries, grad_out)]

    own_kv = stacked(flat[0], flat[1])
    kv_a, kv_b = pair_swap(own_kv, "row", 0), pair_swap(own_kv, "row", 1)
    triple = jax.ShapeDtypeStruct((6 * TILE, feats), bf16)
    kv = call(regroup_kernel, triple, [VMEM] * 3, VMEM)(own_kv, kv_a, kv_b)
    kv_fb, kv_fa = pair_swap(kv, "frame", 1), pair_swap(kv, "frame", 0)
    qg = stacked(flat[2], flat[3])
    qg_late = after(qg, kv)
    qg_a, qg_b = pair_swap(qg_late, "row", 0), pair_swap(qg_late, "row", 1)

    span = TILE // heads
    pair, four = (jax.ShapeDtypeStruct((n, span, feats), bf16) for n in (2, 4))
    near_shape = jax.ShapeDtypeStruct((heads - 1, 2, span, feats), bf16)
    wide = jax.ShapeDtypeStruct((WIDE, feats), bf16)
    attended, stat, column, bias, key_near, value_near = call(
        query_kernel,
        (
            jax.ShapeDtypeStruct((TILE, feats), bf16),
            jax.ShapeDtypeStruct((8, TILE), f32),
            jax.ShapeDtypeStruct((TILE, 128), f32),
            jax.ShapeDtypeStruct((1, WIDE), f32),
            wide,
            wide,
        ),
        [SMEM] + [VMEM] * 5,
        (VMEM,) * 6,
    )(tile_pairs, tile_pairs, qg, kv, kv_fb, kv_fa)
    st_a, st_b = pair_swap(stat, "row", 0), pair_swap(stat, "row", 1)

    def terms(sides, kinds, *kvs):
        row_near = pltpu.VMEM((3 * TILE, feats), bf16)
        return call(
            lambda *refs: key_kernel(sides, *refs),
            [jax.ShapeDtypeStruct((2 * TILE, feats), kind) for kind in kinds],
            [VMEM] * (len(sides) + 6),
            [VMEM] * len(sides),
            [row_near, row_near, pltpu.VMEM((len(sides), 8, 3 * TILE), f32)],
        )(*kvs, qg, qg_a, qg_b, stat, st_a, st_b)

    term_b, term_a = terms((2, 1), (bf16, bf16), kv_fb, kv_fa)
    got_b, got_a = pair_swap(term_b, "frame", 1), pair_swap(term_a, "frame", 0)
    (own,) = terms((0,), (f32,), after(own_kv, got_a))
    far_q, near_q = call(
        lambda *refs: query_grad_kernel(heads, *refs),
        (pair, near_shape),
        [VMEM] * 6,
        (VMEM, VMEM),
    )(after(qg, got_a), key_near, value_near, attended, column, bias)
    got_far_q = head_swap(far_q, heads // 2)

    far_k, *near_k = call(
        lambda *refs: fold_kernel(heads, *refs),
        [pair] + [four] * (heads - 1),
        [VMEM] * 4,
        [VMEM] * heads,
    )(own, got_b, got_a, near_q)
    got_far_k = head_swap(after(far_k, got_far_q), heads // 2)
    got_near = [head_swap(sent, k) for k, sent in zip(near_heads(heads), near_k)]

    out = jax.ShapeDtypeStruct((frames_dev * rows_dev, columns // heads, heads * feats), bf16)
    outs = call(
        lambda *refs: assemble_kernel(heads, *refs),
        [out] * 4,
        [VMEM] * (heads + 1),
        [VMEM] * 4,
    )(got_far_q, got_far_k, *got_near)
    return tuple(x.reshape((frames_dev, rows_dev) + out.shape[1:]) for x in outs)


def solution(mesh):
    inputs = P("frame", "row", None, "head")
    outputs = P("frame", "row", "head", None)
    return jax.shard_map(
        body,
        mesh=mesh,
        in_specs=(inputs,) * 4 + (P("frame", "row", None, None),),
        out_specs=(outputs,) * 4,
        check_vma=False,
    )
```

```python
import jax
import jax.numpy as jnp
from jax import lax
from jax.experimental import pallas as pl
from jax.experimental.pallas import tpu as pltpu
from jax.sharding import PartitionSpec as P

HEAD_DIM = 128
TILE = 192
SLOTS = 9
WIDE = SLOTS * TILE
SCALE = HEAD_DIM**-0.5
SCALE2 = SCALE * 1.4426950408889634
FAR = 1e30
VMEM_LIMIT = 48 * 1024 * 1024

VMEM = pl.BlockSpec(memory_space=pltpu.VMEM)
SMEM = pl.BlockSpec(memory_space=pltpu.SMEM)


def call(kernel, outs, in_specs, out_specs, scratch=()):
    return pl.pallas_call(
        kernel,
        out_shape=outs,
        in_specs=in_specs,
        out_specs=out_specs,
        scratch_shapes=list(scratch),
        compiler_params=pltpu.CompilerParams(vmem_limit_bytes=VMEM_LIMIT),
    )


def pair_swap(value, axis, parity):
    count = lax.axis_size(axis)
    pairs = []
    for low in range(parity, count - 1, 2):
        pairs += [(low, low + 1), (low + 1, low)]
    return lax.ppermute(value, axis, pairs)


def slot_steps(axis):
    near = 1 - 2 * (lax.axis_index(axis) % 2)
    return (0, near, -near)


def slot_offsets():
    return [(a, b) for a in slot_steps("frame") for b in slot_steps("row")]


def regroup_kernel(a_ref, b_ref, rows_ref, far_ref):
    for ref in (rows_ref, far_ref):
        ref[0 : 2 * TILE, :] = a_ref[...]
        ref[2 * TILE : 4 * TILE, :] = b_ref[...]
    far_ref[4 * TILE :, :] = jnp.zeros((16, far_ref.shape[1]), far_ref.dtype)


def gather_near(tiles, first_ref, second_ref):
    for slot, (ref, start) in enumerate(tiles):
        rows = slice(slot * TILE, (slot + 1) * TILE)
        first_ref[rows, :] = ref[start : start + TILE, :]
        second_ref[rows, :] = ref[start + TILE : start + 2 * TILE, :]


def column_blocks(firsts, seconds, heads):
    group, span = 8 // heads, TILE // heads
    me = lax.axis_index("head")
    row = lax.broadcasted_iota(jnp.int32, (TILE, TILE), 0)
    col = lax.broadcasted_iota(jnp.int32, (TILE, TILE), 1)
    block = jnp.zeros_like(row)
    for d in range(1, heads):
        block += (row >= d * span).astype(jnp.int32)
    inner = row - block * span
    shift = group.bit_length() - 1
    source = (inner >> shift) * 8 + (block ^ me) * group + (inner & (group - 1))
    order = (col == source).astype(jnp.bfloat16)
    joined = jnp.concatenate(firsts + seconds, axis=1)
    moved = jnp.dot(order, joined, preferred_element_type=jnp.float32).astype(jnp.bfloat16)
    feats = joined.shape[1] // 2
    return [
        [moved[k * span : (k + 1) * span, i * feats : (i + 1) * feats] for i in range(2)]
        for k in range(heads)
    ]


def near_heads(heads):
    return [k for k in range(heads) if k != heads // 2]


def assemble_kernel(heads, far_q, far_k, *refs):
    near_refs, out_refs = refs[: heads - 1], refs[heads - 1 :]
    feats = far_q.shape[2]
    me = lax.axis_index("head")

    def put(k, i, rows):
        place = pl.ds(pl.multiple_of((me ^ k) * feats, HEAD_DIM), feats)
        out_refs[i][:, :, place] = rows.reshape(out_refs[i].shape[:2] + (feats,))

    for i in range(2):
        put(heads // 2, i, far_q[i])
        put(heads // 2, 2 + i, far_k[i])
    for k, ref in zip(near_heads(heads), near_refs):
        for i in range(4):
            put(k, i, ref[i])


def query_kernel(pairs_s, pairs_v, own_qg, kv, kv_rows, corner_fa, corner_fb, kv_fb, kv_fa, *refs):
    attended_ref, stat_ref, column_ref, bias_ref, key_ref, value_ref = refs
    frame, row = lax.axis_index("frame"), lax.axis_index("row")
    frames, rows = lax.axis_size("frame"), lax.axis_size("row")
    tiles = []
    for own, corners in ((kv, kv_rows), (kv_fa, corner_fa), (kv_fb, corner_fb)):
        tiles += [(own, 0), (corners, 0), (corners, 2 * TILE)]
    gather_near(tiles, key_ref, value_ref)
    lane = lax.broadcasted_iota(jnp.int32, (1, WIDE), 1)
    bias = jnp.zeros((1, WIDE), jnp.float32)
    for slot, (a, b) in enumerate(slot_offsets()):
        bit = pairs_s[0, 0, 0, 9 * (a + 1) + 3 * (b + 1) + 1]
        inside = (frame + a >= 0) & (frame + a < frames) & (row + b >= 0) & (row + b < rows)
        level = jnp.where((bit == 1) & inside, 0.0, -FAR).astype(jnp.float32)
        here = (lane >= slot * TILE) & (lane < (slot + 1) * TILE)
        bias = jnp.where(here, level, bias)
    stat_lane = lax.broadcasted_iota(jnp.int32, (TILE, 128), 1)
    stats = jnp.zeros((TILE, 128), jnp.float32)
    count = own_qg.shape[1] // HEAD_DIM
    for h in range(count):
        feat = slice(h * HEAD_DIM, (h + 1) * HEAD_DIM)
        query, grad = own_qg[0:TILE, feat], own_qg[TILE : 2 * TILE, feat]
        scores = lax.dot_general(
            query, key_ref[:, feat], (((1,), (1,)), ((), ())), preferred_element_type=jnp.float32
        )
        scores = scores * SCALE2 + bias
        top = jnp.max(scores, axis=1, keepdims=True)
        weights = jnp.exp2(scores - top)
        total = jnp.sum(weights, axis=1, keepdims=True)
        rounded = (weights * (1.0 / total)).astype(jnp.bfloat16)
        attended = jnp.dot(rounded, value_ref[:, feat], preferred_element_type=jnp.float32)
        attended = attended.astype(jnp.bfloat16)
        spread = jnp.sum(
            grad.astype(jnp.float32) * attended.astype(jnp.float32), axis=1, keepdims=True
        )
        attended_ref[:, feat] = attended
        stats = jnp.where(stat_lane == h, top + jnp.log2(total), stats)
        stats = jnp.where(stat_lane == count + h, spread, stats)
    bias_ref[...] = bias
    column_ref[...] = stats
    stat_ref[...] = stats.T[0:8, :]
    stat_ref[7:8, 0:27] = pairs_v[0, 0].astype(jnp.float32)


def query_grad_kernel(heads, own_qg, key_ref, value_ref, attended_ref, column_ref, bias_ref, *refs):
    far_ref, near_ref = refs
    bias = bias_ref[...]
    count = own_qg.shape[1] // HEAD_DIM
    grad_parts = []
    for h in range(count):
        feat = slice(h * HEAD_DIM, (h + 1) * HEAD_DIM)
        query, grad = own_qg[0:TILE, feat], own_qg[TILE : 2 * TILE, feat]
        key = key_ref[:, feat]
        scores = lax.dot_general(
            query, key, (((1,), (1,)), ((), ())), preferred_element_type=jnp.float32
        )
        weights = jnp.exp2(scores * SCALE2 + bias - column_ref[:, h : h + 1])
        pushes = lax.dot_general(
            grad, value_ref[:, feat], (((1,), (1,)), ((), ())), preferred_element_type=jnp.float32
        )
        spread = column_ref[:, count + h : count + h + 1]
        slopes = (weights * (pushes - spread)).astype(jnp.bfloat16)
        query_grad = SCALE * jnp.dot(slopes, key, preferred_element_type=jnp.float32)
        grad_parts.append(query_grad.astype(jnp.bfloat16))
    blocks = column_blocks([attended_ref[...]], grad_parts, heads)
    for i in range(2):
        far_ref[i] = blocks[heads // 2][i]
        for at, k in enumerate(near_heads(heads)):
            near_ref[at, i] = blocks[k][i]


def key_kernel(sides, *refs):
    kvs, refs = refs[: len(sides)], refs[len(sides) :]
    (qg, qg_a, qg_b, st, st_a, st_b), refs = refs[:6], refs[6:]
    outs, (query_ref, grad_ref, stat_ref) = refs[: len(sides)], refs[len(sides) :]
    count = qg.shape[1] // HEAD_DIM
    frame, frames = lax.axis_index("frame"), lax.axis_size("frame")
    gather_near([(qg, 0), (qg_a, 0), (qg_b, 0)], query_ref, grad_ref)
    lane = lax.broadcasted_iota(jnp.int32, (1, TILE), 1)
    level = lax.broadcasted_iota(jnp.int32, (8, TILE), 0)
    frame_steps = [slot_steps("frame")[side] for side in sides]
    for slot, (ref, b) in enumerate(zip((st, st_a, st_b), slot_steps("row"))):
        block = ref[...]
        for i, a in enumerate(frame_steps):
            index = 9 * (a + 1) + 3 * (1 - b) + 1
            bit = jnp.sum(jnp.where(lane == index, block[7:8, :], 0.0), axis=1, keepdims=True)
            inside = (frame + a >= 0) & (frame + a < frames)
            bit = bit * jnp.where(inside, 1.0, 0.0).astype(jnp.float32)
            closed = (level < count) & (bit < 0.5)
            stat_ref[i, :, slot * TILE : (slot + 1) * TILE] = jnp.where(closed, FAR, block)
    for h in range(count):
        feat = slice(h * HEAD_DIM, (h + 1) * HEAD_DIM)
        query, grad = query_ref[:, feat], grad_ref[:, feat]
        keys = jnp.concatenate([ref[0:TILE, feat] for ref in kvs], axis=0)
        values = jnp.concatenate([ref[TILE : 2 * TILE, feat] for ref in kvs], axis=0)
        scores = lax.dot_general(
            keys, query, (((1,), (1,)), ((), ())), preferred_element_type=jnp.float32
        )
        pushes = lax.dot_general(
            values, grad, (((1,), (1,)), ((), ())), preferred_element_type=jnp.float32
        )
        rounded, slopes = [], []
        for i in range(len(sides)):
            rows = slice(i * TILE, (i + 1) * TILE)
            weights = jnp.exp2(scores[rows] * SCALE2 - stat_ref[i, h : h + 1, :])
            spread = stat_ref[i, count + h : count + h + 1, :]
            rounded.append(weights.astype(jnp.bfloat16))
            slopes.append((weights * (pushes[rows] - spread)).astype(jnp.bfloat16))
        rounded, slopes = jnp.concatenate(rounded, axis=0), jnp.concatenate(slopes, axis=0)
        value_grad = jnp.dot(rounded, grad, preferred_element_type=jnp.float32)
        key_grad = SCALE * jnp.dot(slopes, query, preferred_element_type=jnp.float32)
        for i, ref in enumerate(outs):
            rows = slice(i * TILE, (i + 1) * TILE)
            if ref.shape[0] > 2 * TILE:
                ref[2 * TILE :, feat] = jnp.zeros((16, HEAD_DIM), ref.dtype)
            ref[0:TILE, feat] = key_grad[rows].astype(ref.dtype)
            ref[TILE : 2 * TILE, feat] = value_grad[rows].astype(ref.dtype)


def fold_kernel(heads, own_ref, got_b, got_a, near_q, far_ref, *near_refs):
    total = own_ref[...] + got_a[...].astype(jnp.float32)
    total += got_b[0 : 2 * TILE, :].astype(jnp.float32)
    total = total.astype(jnp.bfloat16)
    blocks = column_blocks([total[0:TILE]], [total[TILE : 2 * TILE]], heads)
    for i in range(2):
        far_ref[i] = blocks[heads // 2][i]
        for at, (k, ref) in enumerate(zip(near_heads(heads), near_refs)):
            ref[i] = near_q[at, i]
            ref[2 + i] = blocks[k][i]


def after(value, *others):
    return lax.optimization_barrier((value,) + others)[0]


def head_swap(value, k):
    count = lax.axis_size("head")
    return lax.ppermute(value, "head", [(i, i ^ k) for i in range(count)]) if k else value


def stacked(first, second):
    rows = first.shape[0]
    low = jnp.pad(first, ((0, rows), (0, 0)), constant_values=-jnp.inf)
    return jnp.maximum(low, jnp.pad(second, ((rows, 0), (0, 0)), constant_values=-jnp.inf))


def body(queries, key_tokens, value_tokens, grad_out, tile_pairs):
    frames_dev, rows_dev, columns, feats = queries.shape
    heads = lax.axis_size("head")
    bf16, f32 = jnp.bfloat16, jnp.float32
    flat = [x.reshape(TILE, feats) for x in (key_tokens, value_tokens, queries, grad_out)]

    own_kv = stacked(flat[0], flat[1])
    kv_a, kv_b = pair_swap(own_kv, "row", 0), pair_swap(own_kv, "row", 1)
    kv_fb, kv_fa = pair_swap(own_kv, "frame", 1), pair_swap(own_kv, "frame", 0)
    two = [jax.ShapeDtypeStruct((4 * TILE + extra, feats), bf16) for extra in (0, 16)]
    rows, far_rows = call(regroup_kernel, two, [VMEM] * 2, (VMEM, VMEM))(kv_a, kv_b)
    corner_fb = pair_swap(far_rows, "frame", 1)
    corner_fa = pair_swap(after(rows, kv_fb, kv_fa), "frame", 0)
    qg = stacked(flat[2], flat[3])
    qg_late = after(qg, rows)
    qg_a, qg_b = pair_swap(qg_late, "row", 0), pair_swap(qg_late, "row", 1)

    span = TILE // heads
    pair, four = (jax.ShapeDtypeStruct((n, span, feats), bf16) for n in (2, 4))
    near_shape = jax.ShapeDtypeStruct((heads - 1, 2, span, feats), bf16)
    wide = jax.ShapeDtypeStruct((WIDE, feats), bf16)
    attended, stat, column, bias, key_near, value_near = call(
        query_kernel,
        (
            jax.ShapeDtypeStruct((TILE, feats), bf16),
            jax.ShapeDtypeStruct((8, TILE), f32),
            jax.ShapeDtypeStruct((TILE, 128), f32),
            jax.ShapeDtypeStruct((1, WIDE), f32),
            wide,
            wide,
        ),
        [SMEM] + [VMEM] * 8,
        (VMEM,) * 6,
    )(tile_pairs, tile_pairs, qg, own_kv, rows, corner_fa, corner_fb, kv_fb, kv_fa)
    st_a, st_b = pair_swap(stat, "row", 0), pair_swap(stat, "row", 1)

    def terms(sides, kinds, *kvs):
        row_near = pltpu.VMEM((3 * TILE, feats), bf16)
        return call(
            lambda *refs: key_kernel(sides, *refs),
            [jax.ShapeDtypeStruct((2 * TILE + extra, feats), kind) for kind, extra in kinds],
            [VMEM] * (len(sides) + 6),
            [VMEM] * len(sides),
            [row_near, row_near, pltpu.VMEM((len(sides), 8, 3 * TILE), f32)],
        )(*kvs, qg, qg_a, qg_b, stat, st_a, st_b)

    term_b, term_a = terms((2, 1), ((bf16, 16), (bf16, 0)), kv_fb, kv_fa)
    got_b, got_a = pair_swap(term_b, "frame", 1), pair_swap(term_a, "frame", 0)
    (own,) = terms((0,), ((f32, 0),), after(own_kv, got_a))
    far_q, near_q = call(
        lambda *refs: query_grad_kernel(heads, *refs),
        (pair, near_shape),
        [VMEM] * 6,
        (VMEM, VMEM),
    )(after(qg, got_a), key_near, value_near, attended, column, bias)
    got_far_q = head_swap(far_q, heads // 2)

    far_k, *near_k = call(
        lambda *refs: fold_kernel(heads, *refs),
        [pair] + [four] * (heads - 1),
        [VMEM] * 4,
        [VMEM] * heads,
    )(own, got_b, got_a, near_q)
    got_far_k = head_swap(after(far_k, got_far_q), heads // 2)
    got_near = [head_swap(sent, k) for k, sent in zip(near_heads(heads), near_k)]

    out = jax.ShapeDtypeStruct((frames_dev * rows_dev, columns // heads, heads * feats), bf16)
    outs = call(
        lambda *refs: assemble_kernel(heads, *refs),
        [out] * 4,
        [VMEM] * (heads + 1),
        [VMEM] * 4,
    )(got_far_q, got_far_k, *got_near)
    return tuple(x.reshape((frames_dev, rows_dev) + out.shape[1:]) for x in outs)


def solution(mesh):
    inputs = P("frame", "row", None, "head")
    outputs = P("frame", "row", "head", None)
    return jax.shard_map(
        body,
        mesh=mesh,
        in_specs=(inputs,) * 4 + (P("frame", "row", None, None),),
        out_specs=(outputs,) * 4,
        check_vma=False,
    )
```

```python
import jax
import jax.numpy as jnp
from jax import lax
from jax.experimental import pallas as pl
from jax.experimental.pallas import tpu as pltpu
from jax.sharding import PartitionSpec as P

HEAD_DIM = 128
TILE = 192
SLOTS = 9
WIDE = SLOTS * TILE
SCALE = HEAD_DIM**-0.5
SCALE2 = SCALE * 1.4426950408889634
FAR = 1e30
VMEM_LIMIT = 48 * 1024 * 1024

VMEM = pl.BlockSpec(memory_space=pltpu.VMEM)
SMEM = pl.BlockSpec(memory_space=pltpu.SMEM)


def call(kernel, outs, in_specs, out_specs, scratch=()):
    return pl.pallas_call(
        kernel,
        out_shape=outs,
        in_specs=in_specs,
        out_specs=out_specs,
        scratch_shapes=list(scratch),
        compiler_params=pltpu.CompilerParams(vmem_limit_bytes=VMEM_LIMIT),
    )


def pair_swap(value, axis, parity):
    count = lax.axis_size(axis)
    pairs = []
    for low in range(parity, count - 1, 2):
        pairs += [(low, low + 1), (low + 1, low)]
    return lax.ppermute(value, axis, pairs)


def slot_steps(axis):
    near = 1 - 2 * (lax.axis_index(axis) % 2)
    return (0, near, -near)


def slot_offsets():
    return [(a, b) for a in slot_steps("frame") for b in slot_steps("row")]


def regroup_kernel(a_ref, b_ref, rows_ref, far_ref):
    for ref in (rows_ref, far_ref):
        ref[0 : 2 * TILE, :] = a_ref[...]
        ref[2 * TILE : 4 * TILE, :] = b_ref[...]
    far_ref[4 * TILE :, :] = jnp.zeros((16, far_ref.shape[1]), far_ref.dtype)


def gather_near(tiles, first_ref, second_ref):
    for slot, (ref, start) in enumerate(tiles):
        rows = slice(slot * TILE, (slot + 1) * TILE)
        first_ref[rows, :] = ref[start : start + TILE, :]
        second_ref[rows, :] = ref[start + TILE : start + 2 * TILE, :]


def column_blocks(firsts, seconds, heads):
    group, span = 8 // heads, TILE // heads
    me = lax.axis_index("head")
    row = lax.broadcasted_iota(jnp.int32, (TILE, TILE), 0)
    col = lax.broadcasted_iota(jnp.int32, (TILE, TILE), 1)
    block = jnp.zeros_like(row)
    for d in range(1, heads):
        block += (row >= d * span).astype(jnp.int32)
    inner = row - block * span
    shift = group.bit_length() - 1
    source = (inner >> shift) * 8 + (block ^ me) * group + (inner & (group - 1))
    order = (col == source).astype(jnp.bfloat16)
    joined = jnp.concatenate(firsts + seconds, axis=1)
    moved = jnp.dot(order, joined, preferred_element_type=jnp.float32).astype(jnp.bfloat16)
    feats = joined.shape[1] // 2
    return [
        [moved[k * span : (k + 1) * span, i * feats : (i + 1) * feats] for i in range(2)]
        for k in range(heads)
    ]


def far_first(heads):
    return [heads // 2] + [k for k in range(heads) if k != heads // 2]


def assemble_kernel(*refs):
    heads = len(refs) - 4
    got_refs, out_refs = refs[:heads], refs[heads:]
    feats = got_refs[0].shape[2]
    me = lax.axis_index("head")
    for k, ref in zip(far_first(heads), got_refs):
        place = pl.ds(pl.multiple_of((me ^ k) * feats, HEAD_DIM), feats)
        for i, out_ref in enumerate(out_refs):
            out_ref[:, :, place] = ref[i].reshape(out_ref.shape[:2] + (feats,))


def query_kernel(pairs_s, pairs_v, own_qg, kv, kv_rows, corner_fa, corner_fb, kv_fb, kv_fa, *refs):
    attended_ref, stat_ref, column_ref, bias_ref, key_ref, value_ref = refs
    frame, row = lax.axis_index("frame"), lax.axis_index("row")
    frames, rows = lax.axis_size("frame"), lax.axis_size("row")
    tiles = []
    for own, corners in ((kv, kv_rows), (kv_fa, corner_fa), (kv_fb, corner_fb)):
        tiles += [(own, 0), (corners, 0), (corners, 2 * TILE)]
    gather_near(tiles, key_ref, value_ref)
    lane = lax.broadcasted_iota(jnp.int32, (1, WIDE), 1)
    bias = jnp.zeros((1, WIDE), jnp.float32)
    for slot, (a, b) in enumerate(slot_offsets()):
        bit = pairs_s[0, 0, 0, 9 * (a + 1) + 3 * (b + 1) + 1]
        inside = (frame + a >= 0) & (frame + a < frames) & (row + b >= 0) & (row + b < rows)
        level = jnp.where((bit == 1) & inside, 0.0, -FAR).astype(jnp.float32)
        here = (lane >= slot * TILE) & (lane < (slot + 1) * TILE)
        bias = jnp.where(here, level, bias)
    stat_lane = lax.broadcasted_iota(jnp.int32, (TILE, 128), 1)
    stats = jnp.zeros((TILE, 128), jnp.float32)
    count = own_qg.shape[1] // HEAD_DIM
    for h in range(count):
        feat = slice(h * HEAD_DIM, (h + 1) * HEAD_DIM)
        query, grad = own_qg[0:TILE, feat], own_qg[TILE : 2 * TILE, feat]
        scores = lax.dot_general(
            query, key_ref[:, feat], (((1,), (1,)), ((), ())), preferred_element_type=jnp.float32
        )
        scores = scores * SCALE2 + bias
        top = jnp.max(scores, axis=1, keepdims=True)
        weights = jnp.exp2(scores - top)
        total = jnp.sum(weights, axis=1, keepdims=True)
        rounded = (weights * (1.0 / total)).astype(jnp.bfloat16)
        attended = jnp.dot(rounded, value_ref[:, feat], preferred_element_type=jnp.float32)
        attended = attended.astype(jnp.bfloat16)
        spread = jnp.sum(
            grad.astype(jnp.float32) * attended.astype(jnp.float32), axis=1, keepdims=True
        )
        attended_ref[:, feat] = attended
        stats = jnp.where(stat_lane == h, top + jnp.log2(total), stats)
        stats = jnp.where(stat_lane == count + h, spread, stats)
    bias_ref[...] = bias
    column_ref[...] = stats
    stat_ref[...] = stats.T[0:8, :]
    stat_ref[7:8, 0:27] = pairs_v[0, 0].astype(jnp.float32)


def query_grad_kernel(own_qg, key_ref, value_ref, attended_ref, column_ref, bias_ref, send_ref):
    bias = bias_ref[...]
    count = own_qg.shape[1] // HEAD_DIM
    grad_parts = []
    for h in range(count):
        feat = slice(h * HEAD_DIM, (h + 1) * HEAD_DIM)
        query, grad = own_qg[0:TILE, feat], own_qg[TILE : 2 * TILE, feat]
        key = key_ref[:, feat]
        scores = lax.dot_general(
            query, key, (((1,), (1,)), ((), ())), preferred_element_type=jnp.float32
        )
        weights = jnp.exp2(scores * SCALE2 + bias - column_ref[:, h : h + 1])
        pushes = lax.dot_general(
            grad, value_ref[:, feat], (((1,), (1,)), ((), ())), preferred_element_type=jnp.float32
        )
        spread = column_ref[:, count + h : count + h + 1]
        slopes = (weights * (pushes - spread)).astype(jnp.bfloat16)
        query_grad = SCALE * jnp.dot(slopes, key, preferred_element_type=jnp.float32)
        grad_parts.append(query_grad.astype(jnp.bfloat16))
    blocks = column_blocks([attended_ref[...]], grad_parts, send_ref.shape[0])
    for k, pair in enumerate(blocks):
        for i in range(2):
            send_ref[k, i] = pair[i]


def key_kernel(sides, *refs):
    kvs, refs = refs[: len(sides)], refs[len(sides) :]
    (qg, qg_a, qg_b, st, st_a, st_b), refs = refs[:6], refs[6:]
    outs, (query_ref, grad_ref, stat_ref) = refs[: len(sides)], refs[len(sides) :]
    count = qg.shape[1] // HEAD_DIM
    frame, frames = lax.axis_index("frame"), lax.axis_size("frame")
    gather_near([(qg, 0), (qg_a, 0), (qg_b, 0)], query_ref, grad_ref)
    lane = lax.broadcasted_iota(jnp.int32, (1, TILE), 1)
    level = lax.broadcasted_iota(jnp.int32, (8, TILE), 0)
    frame_steps = [slot_steps("frame")[side] for side in sides]
    for slot, (ref, b) in enumerate(zip((st, st_a, st_b), slot_steps("row"))):
        block = ref[...]
        for i, a in enumerate(frame_steps):
            index = 9 * (a + 1) + 3 * (1 - b) + 1
            bit = jnp.sum(jnp.where(lane == index, block[7:8, :], 0.0), axis=1, keepdims=True)
            inside = (frame + a >= 0) & (frame + a < frames)
            bit = bit * jnp.where(inside, 1.0, 0.0).astype(jnp.float32)
            closed = (level < count) & (bit < 0.5)
            stat_ref[i, :, slot * TILE : (slot + 1) * TILE] = jnp.where(closed, FAR, block)
    for h in range(count):
        feat = slice(h * HEAD_DIM, (h + 1) * HEAD_DIM)
        query, grad = query_ref[:, feat], grad_ref[:, feat]
        keys = jnp.concatenate([ref[0:TILE, feat] for ref in kvs], axis=0)
        values = jnp.concatenate([ref[TILE : 2 * TILE, feat] for ref in kvs], axis=0)
        scores = lax.dot_general(
            keys, query, (((1,), (1,)), ((), ())), preferred_element_type=jnp.float32
        )
        pushes = lax.dot_general(
            values, grad, (((1,), (1,)), ((), ())), preferred_element_type=jnp.float32
        )
        rounded, slopes = [], []
        for i in range(len(sides)):
            rows = slice(i * TILE, (i + 1) * TILE)
            weights = jnp.exp2(scores[rows] * SCALE2 - stat_ref[i, h : h + 1, :])
            spread = stat_ref[i, count + h : count + h + 1, :]
            rounded.append(weights.astype(jnp.bfloat16))
            slopes.append((weights * (pushes[rows] - spread)).astype(jnp.bfloat16))
        rounded, slopes = jnp.concatenate(rounded, axis=0), jnp.concatenate(slopes, axis=0)
        value_grad = jnp.dot(rounded, grad, preferred_element_type=jnp.float32)
        key_grad = SCALE * jnp.dot(slopes, query, preferred_element_type=jnp.float32)
        for i, ref in enumerate(outs):
            rows = slice(i * TILE, (i + 1) * TILE)
            if ref.shape[0] > 2 * TILE:
                ref[2 * TILE :, feat] = jnp.zeros((16, HEAD_DIM), ref.dtype)
            ref[0:TILE, feat] = key_grad[rows].astype(ref.dtype)
            ref[TILE : 2 * TILE, feat] = value_grad[rows].astype(ref.dtype)


def fold_kernel(own_ref, got_b, got_a, query_blocks, *send_refs):
    total = own_ref[...] + got_a[...].astype(jnp.float32)
    total += got_b[0 : 2 * TILE, :].astype(jnp.float32)
    total = total.astype(jnp.bfloat16)
    blocks = column_blocks([total[0:TILE]], [total[TILE : 2 * TILE]], len(send_refs))
    for k, ref in enumerate(send_refs):
        for i in range(2):
            ref[i] = query_blocks[k, i]
            ref[2 + i] = blocks[k][i]


def after(value, *others):
    return lax.optimization_barrier((value,) + others)[0]


def head_swap(value, k):
    count = lax.axis_size("head")
    return lax.ppermute(value, "head", [(i, i ^ k) for i in range(count)]) if k else value


def stacked(first, second):
    rows = first.shape[0]
    low = jnp.pad(first, ((0, rows), (0, 0)), constant_values=-jnp.inf)
    return jnp.maximum(low, jnp.pad(second, ((rows, 0), (0, 0)), constant_values=-jnp.inf))


def body(queries, key_tokens, value_tokens, grad_out, tile_pairs):
    frames_dev, rows_dev, columns, feats = queries.shape
    heads = lax.axis_size("head")
    bf16, f32 = jnp.bfloat16, jnp.float32
    flat = [x.reshape(TILE, feats) for x in (key_tokens, value_tokens, queries, grad_out)]

    own_kv = stacked(flat[0], flat[1])
    kv_a, kv_b = pair_swap(own_kv, "row", 0), pair_swap(own_kv, "row", 1)
    kv_fb, kv_fa = pair_swap(own_kv, "frame", 1), pair_swap(own_kv, "frame", 0)
    qg = stacked(flat[2], flat[3])
    two = [jax.ShapeDtypeStruct((4 * TILE + extra, feats), bf16) for extra in (0, 16)]
    rows, far_rows = call(regroup_kernel, two, [VMEM] * 2, (VMEM, VMEM))(after(kv_a, qg), kv_b)
    corner_fb = pair_swap(far_rows, "frame", 1)
    corner_fa = pair_swap(after(rows, kv_fb, kv_fa), "frame", 0)
    qg_late = after(qg, rows)
    qg_a, qg_b = pair_swap(qg_late, "row", 0), pair_swap(qg_late, "row", 1)

    span = TILE // heads
    wide = jax.ShapeDtypeStruct((WIDE, feats), bf16)
    attended, stat, column, bias, key_near, value_near = call(
        query_kernel,
        (
            jax.ShapeDtypeStruct((TILE, feats), bf16),
            jax.ShapeDtypeStruct((8, TILE), f32),
            jax.ShapeDtypeStruct((TILE, 128), f32),
            jax.ShapeDtypeStruct((1, WIDE), f32),
            wide,
            wide,
        ),
        [SMEM] + [VMEM] * 8,
        (VMEM,) * 6,
    )(tile_pairs, tile_pairs, qg, own_kv, rows, corner_fa, corner_fb, kv_fb, kv_fa)
    st_a, st_b = pair_swap(stat, "row", 0), pair_swap(stat, "row", 1)

    def terms(sides, kinds, *kvs):
        row_near = pltpu.VMEM((3 * TILE, feats), bf16)
        return call(
            lambda *refs: key_kernel(sides, *refs),
            [jax.ShapeDtypeStruct((2 * TILE + extra, feats), kind) for kind, extra in kinds],
            [VMEM] * (len(sides) + 6),
            [VMEM] * len(sides),
            [row_near, row_near, pltpu.VMEM((len(sides), 8, 3 * TILE), f32)],
        )(*kvs, qg, qg_a, qg_b, stat, st_a, st_b)

    term_b, term_a = terms((2, 1), ((bf16, 16), (bf16, 0)), kv_fb, kv_fa)
    got_b, got_a = pair_swap(term_b, "frame", 1), pair_swap(term_a, "frame", 0)
    (own,) = terms((0,), ((f32, 0),), after(own_kv, got_a))
    sent_q = call(
        query_grad_kernel,
        jax.ShapeDtypeStruct((heads, 2, span, feats), bf16),
        [VMEM] * 6,
        VMEM,
    )(after(qg, got_a), key_near, value_near, attended, column, bias)
    sent = call(
        fold_kernel,
        [jax.ShapeDtypeStruct((4, span, feats), bf16)] * heads,
        [VMEM] * 4,
        [VMEM] * heads,
    )(own, got_b, got_a, sent_q)
    got = [head_swap(sent[k], k) for k in far_first(heads)]

    out = jax.ShapeDtypeStruct((frames_dev * rows_dev, columns // heads, heads * feats), bf16)
    outs = call(assemble_kernel, [out] * 4, [VMEM] * heads, [VMEM] * 4)(*got)
    return tuple(x.reshape((frames_dev, rows_dev) + out.shape[1:]) for x in outs)


def solution(mesh):
    inputs = P("frame", "row", None, "head")
    outputs = P("frame", "row", "head", None)
    return jax.shard_map(
        body,
        mesh=mesh,
        in_specs=(inputs,) * 4 + (P("frame", "row", None, None),),
        out_specs=(outputs,) * 4,
        check_vma=False,
    )
```

```python
import jax
import jax.numpy as jnp
from jax import lax
from jax.experimental import pallas as pl
from jax.experimental.pallas import tpu as pltpu
from jax.sharding import PartitionSpec as P

HEAD_DIM = 128
TILE = 192
SLOTS = 9
WIDE = SLOTS * TILE
SCALE = HEAD_DIM**-0.5
SCALE2 = SCALE * 1.4426950408889634
FAR = 1e30
VMEM_LIMIT = 48 * 1024 * 1024

VMEM = pl.BlockSpec(memory_space=pltpu.VMEM)
SMEM = pl.BlockSpec(memory_space=pltpu.SMEM)


def call(kernel, outs, in_specs, out_specs, scratch=()):
    return pl.pallas_call(
        kernel,
        out_shape=outs,
        in_specs=in_specs,
        out_specs=out_specs,
        scratch_shapes=list(scratch),
        compiler_params=pltpu.CompilerParams(vmem_limit_bytes=VMEM_LIMIT),
    )


def pair_swap(value, axis, parity):
    count = lax.axis_size(axis)
    pairs = []
    for low in range(parity, count - 1, 2):
        pairs += [(low, low + 1), (low + 1, low)]
    return lax.ppermute(value, axis, pairs)


def slot_steps(axis):
    near = 1 - 2 * (lax.axis_index(axis) % 2)
    return (0, near, -near)


def slot_offsets():
    return [(a, b) for a in slot_steps("frame") for b in slot_steps("row")]


def regroup_kernel(a_ref, b_ref, rows_ref, far_ref):
    for ref in (rows_ref, far_ref):
        ref[0 : 2 * TILE, :] = a_ref[...]
        ref[2 * TILE : 4 * TILE, :] = b_ref[...]
    far_ref[4 * TILE :, :] = jnp.zeros((16, far_ref.shape[1]), far_ref.dtype)


def gather_near(tiles, first_ref, second_ref):
    for slot, (ref, start) in enumerate(tiles):
        rows = slice(slot * TILE, (slot + 1) * TILE)
        first_ref[rows, :] = ref[start : start + TILE, :]
        second_ref[rows, :] = ref[start + TILE : start + 2 * TILE, :]


def column_blocks(firsts, seconds, heads):
    group, span = 8 // heads, TILE // heads
    me = lax.axis_index("head")
    row = lax.broadcasted_iota(jnp.int32, (TILE, TILE), 0)
    col = lax.broadcasted_iota(jnp.int32, (TILE, TILE), 1)
    block = jnp.zeros_like(row)
    for d in range(1, heads):
        block += (row >= d * span).astype(jnp.int32)
    inner = row - block * span
    shift = group.bit_length() - 1
    source = (inner >> shift) * 8 + (block ^ me) * group + (inner & (group - 1))
    order = (col == source).astype(jnp.bfloat16)
    joined = jnp.concatenate(firsts + seconds, axis=1)
    moved = jnp.dot(order, joined, preferred_element_type=jnp.float32).astype(jnp.bfloat16)
    feats = joined.shape[1] // 2
    return [
        [moved[k * span : (k + 1) * span, i * feats : (i + 1) * feats] for i in range(2)]
        for k in range(heads)
    ]


def far_first(heads):
    return [heads // 2] + [k for k in reversed(range(heads)) if k != heads // 2]


def assemble_kernel(*refs):
    heads = len(refs) - 4
    got_refs, out_refs = refs[:heads], refs[heads:]
    feats = got_refs[0].shape[2]
    me = lax.axis_index("head")
    for k, ref in zip(far_first(heads), got_refs):
        place = pl.ds(pl.multiple_of((me ^ k) * feats, HEAD_DIM), feats)
        for i, out_ref in enumerate(out_refs):
            out_ref[:, :, place] = ref[i].reshape(out_ref.shape[:2] + (feats,))


def query_kernel(pairs_s, pairs_v, own_qg, kv, kv_rows, corner_fa, corner_fb, kv_fb, kv_fa, *refs):
    attended_ref, stat_ref, column_ref, bias_ref, key_ref, value_ref = refs
    frame, row = lax.axis_index("frame"), lax.axis_index("row")
    frames, rows = lax.axis_size("frame"), lax.axis_size("row")
    tiles = []
    for own, corners in ((kv, kv_rows), (kv_fa, corner_fa), (kv_fb, corner_fb)):
        tiles += [(own, 0), (corners, 0), (corners, 2 * TILE)]
    gather_near(tiles, key_ref, value_ref)
    lane = lax.broadcasted_iota(jnp.int32, (1, WIDE), 1)
    bias = jnp.zeros((1, WIDE), jnp.float32)
    for slot, (a, b) in enumerate(slot_offsets()):
        bit = pairs_s[0, 0, 0, 9 * (a + 1) + 3 * (b + 1) + 1]
        inside = (frame + a >= 0) & (frame + a < frames) & (row + b >= 0) & (row + b < rows)
        level = jnp.where((bit == 1) & inside, 0.0, -FAR).astype(jnp.float32)
        here = (lane >= slot * TILE) & (lane < (slot + 1) * TILE)
        bias = jnp.where(here, level, bias)
    stat_lane = lax.broadcasted_iota(jnp.int32, (TILE, 128), 1)
    stats = jnp.zeros((TILE, 128), jnp.float32)
    count = own_qg.shape[1] // HEAD_DIM
    for h in range(count):
        feat = slice(h * HEAD_DIM, (h + 1) * HEAD_DIM)
        query, grad = own_qg[0:TILE, feat], own_qg[TILE : 2 * TILE, feat]
        scores = lax.dot_general(
            query, key_ref[:, feat], (((1,), (1,)), ((), ())), preferred_element_type=jnp.float32
        )
        scores = scores * SCALE2 + bias
        top = jnp.max(scores, axis=1, keepdims=True)
        weights = jnp.exp2(scores - top)
        total = jnp.sum(weights, axis=1, keepdims=True)
        rounded = (weights * (1.0 / total)).astype(jnp.bfloat16)
        attended = jnp.dot(rounded, value_ref[:, feat], preferred_element_type=jnp.float32)
        attended = attended.astype(jnp.bfloat16)
        spread = jnp.sum(
            grad.astype(jnp.float32) * attended.astype(jnp.float32), axis=1, keepdims=True
        )
        attended_ref[:, feat] = attended
        stats = jnp.where(stat_lane == h, top + jnp.log2(total), stats)
        stats = jnp.where(stat_lane == count + h, spread, stats)
    bias_ref[...] = bias
    column_ref[...] = stats
    stat_ref[...] = stats.T[0:8, :]
    stat_ref[7:8, 0:27] = pairs_v[0, 0].astype(jnp.float32)


def query_grad_kernel(own_qg, key_ref, value_ref, attended_ref, column_ref, bias_ref, send_ref):
    bias = bias_ref[...]
    count = own_qg.shape[1] // HEAD_DIM
    grad_parts = []
    for h in range(count):
        feat = slice(h * HEAD_DIM, (h + 1) * HEAD_DIM)
        query, grad = own_qg[0:TILE, feat], own_qg[TILE : 2 * TILE, feat]
        key = key_ref[:, feat]
        scores = lax.dot_general(
            query, key, (((1,), (1,)), ((), ())), preferred_element_type=jnp.float32
        )
        weights = jnp.exp2(scores * SCALE2 + bias - column_ref[:, h : h + 1])
        pushes = lax.dot_general(
            grad, value_ref[:, feat], (((1,), (1,)), ((), ())), preferred_element_type=jnp.float32
        )
        spread = column_ref[:, count + h : count + h + 1]
        slopes = (weights * (pushes - spread)).astype(jnp.bfloat16)
        query_grad = SCALE * jnp.dot(slopes, key, preferred_element_type=jnp.float32)
        grad_parts.append(query_grad.astype(jnp.bfloat16))
    blocks = column_blocks([attended_ref[...]], grad_parts, send_ref.shape[0])
    for k, pair in enumerate(blocks):
        for i in range(2):
            send_ref[k, i] = pair[i]


def key_kernel(sides, *refs):
    kvs, refs = refs[: len(sides)], refs[len(sides) :]
    (qg, qg_b, qg_a, st, st_a, st_b), refs = refs[:6], refs[6:]
    outs, (query_ref, grad_ref, stat_ref) = refs[: len(sides)], refs[len(sides) :]
    count = qg.shape[1] // HEAD_DIM
    frame, frames = lax.axis_index("frame"), lax.axis_size("frame")
    gather_near([(qg, 0), (qg_a, 0), (qg_b, 0)], query_ref, grad_ref)
    lane = lax.broadcasted_iota(jnp.int32, (1, TILE), 1)
    level = lax.broadcasted_iota(jnp.int32, (8, TILE), 0)
    frame_steps = [slot_steps("frame")[side] for side in sides]
    for slot, (ref, b) in enumerate(zip((st, st_a, st_b), slot_steps("row"))):
        block = ref[...]
        for i, a in enumerate(frame_steps):
            index = 9 * (a + 1) + 3 * (1 - b) + 1
            bit = jnp.sum(jnp.where(lane == index, block[7:8, :], 0.0), axis=1, keepdims=True)
            inside = (frame + a >= 0) & (frame + a < frames)
            bit = bit * jnp.where(inside, 1.0, 0.0).astype(jnp.float32)
            closed = (level < count) & (bit < 0.5)
            stat_ref[i, :, slot * TILE : (slot + 1) * TILE] = jnp.where(closed, FAR, block)
    for h in range(count):
        feat = slice(h * HEAD_DIM, (h + 1) * HEAD_DIM)
        query, grad = query_ref[:, feat], grad_ref[:, feat]
        keys = jnp.concatenate([ref[0:TILE, feat] for ref in kvs], axis=0)
        values = jnp.concatenate([ref[TILE : 2 * TILE, feat] for ref in kvs], axis=0)
        scores = lax.dot_general(
            keys, query, (((1,), (1,)), ((), ())), preferred_element_type=jnp.float32
        )
        pushes = lax.dot_general(
            values, grad, (((1,), (1,)), ((), ())), preferred_element_type=jnp.float32
        )
        rounded, slopes = [], []
        for i in range(len(sides)):
            rows = slice(i * TILE, (i + 1) * TILE)
            weights = jnp.exp2(scores[rows] * SCALE2 - stat_ref[i, h : h + 1, :])
            spread = stat_ref[i, count + h : count + h + 1, :]
            rounded.append(weights.astype(jnp.bfloat16))
            slopes.append((weights * (pushes[rows] - spread)).astype(jnp.bfloat16))
        rounded, slopes = jnp.concatenate(rounded, axis=0), jnp.concatenate(slopes, axis=0)
        value_grad = jnp.dot(rounded, grad, preferred_element_type=jnp.float32)
        key_grad = SCALE * jnp.dot(slopes, query, preferred_element_type=jnp.float32)
        for i, ref in enumerate(outs):
            rows = slice(i * TILE, (i + 1) * TILE)
            if ref.shape[0] > 2 * TILE:
                ref[2 * TILE :, feat] = jnp.zeros((16, HEAD_DIM), ref.dtype)
            ref[0:TILE, feat] = key_grad[rows].astype(ref.dtype)
            ref[TILE : 2 * TILE, feat] = value_grad[rows].astype(ref.dtype)


def fold_kernel(own_ref, got_b, got_a, query_blocks, *send_refs):
    total = own_ref[...] + got_a[...].astype(jnp.float32)
    total += got_b[0 : 2 * TILE, :].astype(jnp.float32)
    total = total.astype(jnp.bfloat16)
    blocks = column_blocks([total[0:TILE]], [total[TILE : 2 * TILE]], len(send_refs))
    for k, ref in enumerate(send_refs):
        for i in range(2):
            ref[i] = query_blocks[k, i]
            ref[2 + i] = blocks[k][i]


def after(value, *others):
    return lax.optimization_barrier((value,) + others)[0]


def head_swap(value, k):
    count = lax.axis_size("head")
    return lax.ppermute(value, "head", [(i, i ^ k) for i in range(count)]) if k else value


def stacked(first, second):
    rows = first.shape[0]
    low = jnp.pad(first, ((0, rows), (0, 0)), constant_values=-jnp.inf)
    return jnp.maximum(low, jnp.pad(second, ((rows, 0), (0, 0)), constant_values=-jnp.inf))


def body(queries, key_tokens, value_tokens, grad_out, tile_pairs):
    frames_dev, rows_dev, columns, feats = queries.shape
    heads = lax.axis_size("head")
    bf16, f32 = jnp.bfloat16, jnp.float32
    flat = [x.reshape(TILE, feats) for x in (key_tokens, value_tokens, queries, grad_out)]

    own_kv = stacked(flat[0], flat[1])
    kv_a, kv_b = pair_swap(own_kv, "row", 0), pair_swap(own_kv, "row", 1)
    kv_fb, kv_fa = pair_swap(own_kv, "frame", 1), pair_swap(own_kv, "frame", 0)
    qg = stacked(flat[2], flat[3])
    two = [jax.ShapeDtypeStruct((4 * TILE + extra, feats), bf16) for extra in (0, 16)]
    rows, far_rows = call(regroup_kernel, two, [VMEM] * 2, (VMEM, VMEM))(after(kv_a, qg), kv_b)
    corner_fb = pair_swap(far_rows, "frame", 1)
    corner_fa = pair_swap(after(rows, kv_fb, kv_fa), "frame", 0)
    qg_late = after(qg, rows)
    qg_b, qg_a = pair_swap(qg_late, "row", 1), pair_swap(qg_late, "row", 0)

    span = TILE // heads
    wide = jax.ShapeDtypeStruct((WIDE, feats), bf16)
    attended, stat, column, bias, key_near, value_near = call(
        query_kernel,
        (
            jax.ShapeDtypeStruct((TILE, feats), bf16),
            jax.ShapeDtypeStruct((8, TILE), f32),
            jax.ShapeDtypeStruct((TILE, 128), f32),
            jax.ShapeDtypeStruct((1, WIDE), f32),
            wide,
            wide,
        ),
        [SMEM] + [VMEM] * 8,
        (VMEM,) * 6,
    )(tile_pairs, tile_pairs, qg, own_kv, rows, corner_fa, corner_fb, kv_fb, kv_fa)
    st_a, st_b = pair_swap(stat, "row", 0), pair_swap(stat, "row", 1)

    def terms(sides, kinds, *kvs):
        row_near = pltpu.VMEM((3 * TILE, feats), bf16)
        return call(
            lambda *refs: key_kernel(sides, *refs),
            [jax.ShapeDtypeStruct((2 * TILE + extra, feats), kind) for kind, extra in kinds],
            [VMEM] * (len(sides) + 6),
            [VMEM] * len(sides),
            [row_near, row_near, pltpu.VMEM((len(sides), 8, 3 * TILE), f32)],
        )(*kvs, qg, qg_b, qg_a, stat, st_a, st_b)

    term_b, term_a = terms((2, 1), ((bf16, 16), (bf16, 0)), kv_fb, kv_fa)
    got_b, got_a = pair_swap(term_b, "frame", 1), pair_swap(term_a, "frame", 0)
    (own,) = terms((0,), ((f32, 0),), after(own_kv, got_a))
    sent_q = call(
        query_grad_kernel,
        jax.ShapeDtypeStruct((heads, 2, span, feats), bf16),
        [VMEM] * 6,
        VMEM,
    )(after(qg, got_a), key_near, value_near, attended, column, bias)
    sent = call(
        fold_kernel,
        [jax.ShapeDtypeStruct((4, span, feats), bf16)] * heads,
        [VMEM] * 4,
        [VMEM] * heads,
    )(own, got_b, got_a, sent_q)
    got = [head_swap(sent[k], k) for k in far_first(heads)]

    out = jax.ShapeDtypeStruct((frames_dev * rows_dev, columns // heads, heads * feats), bf16)
    outs = call(assemble_kernel, [out] * 4, [VMEM] * heads, [VMEM] * 4)(*got)
    return tuple(x.reshape((frames_dev, rows_dev) + out.shape[1:]) for x in outs)


def solution(mesh):
    inputs = P("frame", "row", None, "head")
    outputs = P("frame", "row", "head", None)
    return jax.shard_map(
        body,
        mesh=mesh,
        in_specs=(inputs,) * 4 + (P("frame", "row", None, None),),
        out_specs=(outputs,) * 4,
        check_vma=False,
    )
```

```python
import jax
import jax.numpy as jnp
from jax import lax
from jax.experimental import pallas as pl
from jax.experimental.pallas import tpu as pltpu
from jax.sharding import PartitionSpec as P

HEAD_DIM = 128
TILE = 192
SLOTS = 9
WIDE = SLOTS * TILE
SCALE = HEAD_DIM**-0.5
SCALE2 = SCALE * 1.4426950408889634
FAR = 1e30
VMEM_LIMIT = 48 * 1024 * 1024

VMEM = pl.BlockSpec(memory_space=pltpu.VMEM)
SMEM = pl.BlockSpec(memory_space=pltpu.SMEM)


def call(kernel, outs, in_specs, out_specs, scratch=()):
    return pl.pallas_call(
        kernel,
        out_shape=outs,
        in_specs=in_specs,
        out_specs=out_specs,
        scratch_shapes=list(scratch),
        compiler_params=pltpu.CompilerParams(vmem_limit_bytes=VMEM_LIMIT),
    )


def pair_swap(value, axis, parity):
    count = lax.axis_size(axis)
    pairs = []
    for low in range(parity, count - 1, 2):
        pairs += [(low, low + 1), (low + 1, low)]
    return lax.ppermute(value, axis, pairs)


def slot_steps(axis):
    near = 1 - 2 * (lax.axis_index(axis) % 2)
    return (0, near, -near)


def slot_offsets():
    return [(a, b) for a in slot_steps("frame") for b in slot_steps("row")]


def regroup_kernel(a_ref, b_ref, rows_ref, far_ref):
    for ref in (rows_ref, far_ref):
        ref[0 : 2 * TILE, :] = a_ref[...]
        ref[2 * TILE : 4 * TILE, :] = b_ref[...]
    far_ref[4 * TILE :, :] = jnp.zeros((16, far_ref.shape[1]), far_ref.dtype)


def gather_near(tiles, first_ref, second_ref):
    for slot, (ref, start) in enumerate(tiles):
        rows = slice(slot * TILE, (slot + 1) * TILE)
        first_ref[rows, :] = ref[start : start + TILE, :]
        second_ref[rows, :] = ref[start + TILE : start + 2 * TILE, :]


def column_blocks(firsts, seconds, heads):
    group, span = 8 // heads, TILE // heads
    me = lax.axis_index("head")
    row = lax.broadcasted_iota(jnp.int32, (TILE, TILE), 0)
    col = lax.broadcasted_iota(jnp.int32, (TILE, TILE), 1)
    block = jnp.zeros_like(row)
    for d in range(1, heads):
        block += (row >= d * span).astype(jnp.int32)
    inner = row - block * span
    shift = group.bit_length() - 1
    source = (inner >> shift) * 8 + (block ^ me) * group + (inner & (group - 1))
    order = (col == source).astype(jnp.bfloat16)
    joined = jnp.concatenate(firsts + seconds, axis=1)
    moved = jnp.dot(order, joined, preferred_element_type=jnp.float32).astype(jnp.bfloat16)
    feats = joined.shape[1] // 2
    return [
        [moved[k * span : (k + 1) * span, i * feats : (i + 1) * feats] for i in range(2)]
        for k in range(heads)
    ]


def far_first(heads):
    return [heads // 2] + [k for k in reversed(range(heads)) if k != heads // 2]


def assemble_kernel(*refs):
    heads = len(refs) - 4
    got_refs, out_refs = refs[:heads], refs[heads:]
    feats = got_refs[0].shape[2]
    me = lax.axis_index("head")
    for k, ref in zip(far_first(heads), got_refs):
        place = pl.ds(pl.multiple_of((me ^ k) * feats, HEAD_DIM), feats)
        for i, out_ref in enumerate(out_refs):
            out_ref[:, :, place] = ref[i].reshape(out_ref.shape[:2] + (feats,))


def query_kernel(pairs_s, pairs_v, own_qg, kv, kv_rows, corner_fa, corner_fb, kv_fb, kv_fa, *refs):
    attended_ref, stat_ref, column_ref, bias_ref, key_ref, value_ref = refs
    frame, row = lax.axis_index("frame"), lax.axis_index("row")
    frames, rows = lax.axis_size("frame"), lax.axis_size("row")
    tiles = []
    for own, corners in ((kv, kv_rows), (kv_fa, corner_fa), (kv_fb, corner_fb)):
        tiles += [(own, 0), (corners, 0), (corners, 2 * TILE)]
    gather_near(tiles, key_ref, value_ref)
    lane = lax.broadcasted_iota(jnp.int32, (1, WIDE), 1)
    bias = jnp.zeros((1, WIDE), jnp.float32)
    for slot, (a, b) in enumerate(slot_offsets()):
        bit = pairs_s[0, 0, 0, 9 * (a + 1) + 3 * (b + 1) + 1]
        inside = (frame + a >= 0) & (frame + a < frames) & (row + b >= 0) & (row + b < rows)
        level = jnp.where((bit == 1) & inside, 0.0, -FAR).astype(jnp.float32)
        here = (lane >= slot * TILE) & (lane < (slot + 1) * TILE)
        bias = jnp.where(here, level, bias)
    stat_lane = lax.broadcasted_iota(jnp.int32, (TILE, 128), 1)
    stats = jnp.zeros((TILE, 128), jnp.float32)
    count = own_qg.shape[1] // HEAD_DIM
    for h in range(count):
        feat = slice(h * HEAD_DIM, (h + 1) * HEAD_DIM)
        query, grad = own_qg[0:TILE, feat], own_qg[TILE : 2 * TILE, feat]
        scores = lax.dot_general(
            query, key_ref[:, feat], (((1,), (1,)), ((), ())), preferred_element_type=jnp.float32
        )
        scores = scores * SCALE2 + bias
        top = jnp.max(scores, axis=1, keepdims=True)
        weights = jnp.exp2(scores - top)
        total = jnp.sum(weights, axis=1, keepdims=True)
        rounded = (weights * (1.0 / total)).astype(jnp.bfloat16)
        attended = jnp.dot(rounded, value_ref[:, feat], preferred_element_type=jnp.float32)
        attended = attended.astype(jnp.bfloat16)
        spread = jnp.sum(
            grad.astype(jnp.float32) * attended.astype(jnp.float32), axis=1, keepdims=True
        )
        attended_ref[:, feat] = attended
        stats = jnp.where(stat_lane == h, top + jnp.log2(total), stats)
        stats = jnp.where(stat_lane == count + h, spread, stats)
    bias_ref[...] = bias
    column_ref[...] = stats
    stat_ref[...] = stats.T[0:8, :]
    stat_ref[7:8, 0:27] = pairs_v[0, 0].astype(jnp.float32)


def query_grad_kernel(own_qg, key_ref, value_ref, attended_ref, column_ref, bias_ref, send_ref):
    bias = bias_ref[...]
    count = own_qg.shape[1] // HEAD_DIM
    grad_parts = []
    for h in range(count):
        feat = slice(h * HEAD_DIM, (h + 1) * HEAD_DIM)
        query, grad = own_qg[0:TILE, feat], own_qg[TILE : 2 * TILE, feat]
        key = key_ref[:, feat]
        scores = lax.dot_general(
            query, key, (((1,), (1,)), ((), ())), preferred_element_type=jnp.float32
        )
        weights = jnp.exp2(scores * SCALE2 + bias - column_ref[:, h : h + 1])
        pushes = lax.dot_general(
            grad, value_ref[:, feat], (((1,), (1,)), ((), ())), preferred_element_type=jnp.float32
        )
        spread = column_ref[:, count + h : count + h + 1]
        slopes = (weights * (pushes - spread)).astype(jnp.bfloat16)
        query_grad = SCALE * jnp.dot(slopes, key, preferred_element_type=jnp.float32)
        grad_parts.append(query_grad.astype(jnp.bfloat16))
    blocks = column_blocks([attended_ref[...]], grad_parts, send_ref.shape[0])
    for k, pair in enumerate(blocks):
        for i in range(2):
            send_ref[k, i] = pair[i]


def key_kernel(sides, *refs):
    kvs, refs = refs[: len(sides)], refs[len(sides) :]
    (qg, qg_b, qg_a, st, st_a, st_b), refs = refs[:6], refs[6:]
    outs, (query_ref, grad_ref, stat_ref) = refs[: len(sides)], refs[len(sides) :]
    count = qg.shape[1] // HEAD_DIM
    frame, frames = lax.axis_index("frame"), lax.axis_size("frame")
    gather_near([(qg, 0), (qg_a, 0), (qg_b, 0)], query_ref, grad_ref)
    lane = lax.broadcasted_iota(jnp.int32, (1, TILE), 1)
    level = lax.broadcasted_iota(jnp.int32, (8, TILE), 0)
    frame_steps = [slot_steps("frame")[side] for side in sides]
    for slot, (ref, b) in enumerate(zip((st, st_a, st_b), slot_steps("row"))):
        block = ref[...]
        for i, a in enumerate(frame_steps):
            index = 9 * (a + 1) + 3 * (1 - b) + 1
            bit = jnp.sum(jnp.where(lane == index, block[7:8, :], 0.0), axis=1, keepdims=True)
            inside = (frame + a >= 0) & (frame + a < frames)
            bit = bit * jnp.where(inside, 1.0, 0.0).astype(jnp.float32)
            closed = (level < count) & (bit < 0.5)
            stat_ref[i, :, slot * TILE : (slot + 1) * TILE] = jnp.where(closed, FAR, block)
    for h in range(count):
        feat = slice(h * HEAD_DIM, (h + 1) * HEAD_DIM)
        query, grad = query_ref[:, feat], grad_ref[:, feat]
        keys = jnp.concatenate([ref[0:TILE, feat] for ref in kvs], axis=0)
        values = jnp.concatenate([ref[TILE : 2 * TILE, feat] for ref in kvs], axis=0)
        scores = lax.dot_general(
            keys, query, (((1,), (1,)), ((), ())), preferred_element_type=jnp.float32
        )
        pushes = lax.dot_general(
            values, grad, (((1,), (1,)), ((), ())), preferred_element_type=jnp.float32
        )
        rounded, slopes = [], []
        for i in range(len(sides)):
            rows = slice(i * TILE, (i + 1) * TILE)
            weights = jnp.exp2(scores[rows] * SCALE2 - stat_ref[i, h : h + 1, :])
            spread = stat_ref[i, count + h : count + h + 1, :]
            rounded.append(weights.astype(jnp.bfloat16))
            slopes.append((weights * (pushes[rows] - spread)).astype(jnp.bfloat16))
        rounded, slopes = jnp.concatenate(rounded, axis=0), jnp.concatenate(slopes, axis=0)
        value_grad = jnp.dot(rounded, grad, preferred_element_type=jnp.float32)
        key_grad = SCALE * jnp.dot(slopes, query, preferred_element_type=jnp.float32)
        for i, ref in enumerate(outs):
            rows = slice(i * TILE, (i + 1) * TILE)
            if ref.shape[0] > 2 * TILE:
                ref[2 * TILE :, feat] = jnp.zeros((16, HEAD_DIM), ref.dtype)
            ref[0:TILE, feat] = key_grad[rows].astype(ref.dtype)
            ref[TILE : 2 * TILE, feat] = value_grad[rows].astype(ref.dtype)


def fold_kernel(own_ref, got_b, got_a, query_blocks, *send_refs):
    total = own_ref[...] + got_a[...].astype(jnp.float32)
    total += got_b[0 : 2 * TILE, :].astype(jnp.float32)
    total = total.astype(jnp.bfloat16)
    blocks = column_blocks([total[0:TILE]], [total[TILE : 2 * TILE]], len(send_refs))
    for k, ref in enumerate(send_refs):
        for i in range(2):
            ref[i] = query_blocks[k, i]
            ref[2 + i] = blocks[k][i]


def after(value, *others):
    return lax.optimization_barrier((value,) + others)[0]


def head_swap(value, k):
    count = lax.axis_size("head")
    return lax.ppermute(value, "head", [(i, i ^ k) for i in range(count)]) if k else value


def stacked(first, second):
    rows = first.shape[0]
    low = jnp.pad(first, ((0, rows), (0, 0)), constant_values=-jnp.inf)
    return jnp.maximum(low, jnp.pad(second, ((rows, 0), (0, 0)), constant_values=-jnp.inf))


def body(queries, key_tokens, value_tokens, grad_out, tile_pairs):
    frames_dev, rows_dev, columns, feats = queries.shape
    heads = lax.axis_size("head")
    bf16, f32 = jnp.bfloat16, jnp.float32
    flat = [x.reshape(TILE, feats) for x in (key_tokens, value_tokens, queries, grad_out)]

    own_kv = stacked(flat[0], flat[1])
    kv_a, kv_b = pair_swap(own_kv, "row", 0), pair_swap(own_kv, "row", 1)
    kv_fb, kv_fa = pair_swap(own_kv, "frame", 1), pair_swap(own_kv, "frame", 0)
    qg = stacked(flat[2], flat[3])
    two = [jax.ShapeDtypeStruct((4 * TILE + extra, feats), bf16) for extra in (0, 16)]
    rows, far_rows = call(regroup_kernel, two, [VMEM] * 2, (VMEM, VMEM))(after(kv_a, qg), kv_b)
    corner_fb = pair_swap(far_rows, "frame", 1)
    corner_fa = pair_swap(after(rows, kv_fb, kv_fa), "frame", 0)
    qg_late = after(qg, rows)
    qg_b, qg_a = pair_swap(qg_late, "row", 1), pair_swap(qg_late, "row", 0)

    span = TILE // heads
    wide = jax.ShapeDtypeStruct((WIDE, feats), bf16)
    attended, stat, column, bias, key_near, value_near = call(
        query_kernel,
        (
            jax.ShapeDtypeStruct((TILE, feats), bf16),
            jax.ShapeDtypeStruct((8, TILE), f32),
            jax.ShapeDtypeStruct((TILE, 128), f32),
            jax.ShapeDtypeStruct((1, WIDE), f32),
            wide,
            wide,
        ),
        [SMEM] + [VMEM] * 8,
        (VMEM,) * 6,
    )(tile_pairs, tile_pairs, qg, own_kv, rows, corner_fa, corner_fb, kv_fb, kv_fa)
    st_a, st_b = pair_swap(stat, "row", 0), pair_swap(stat, "row", 1)

    def terms(sides, kinds, *kvs):
        row_near = pltpu.VMEM((3 * TILE, feats), bf16)
        return call(
            lambda *refs: key_kernel(sides, *refs),
            [jax.ShapeDtypeStruct((2 * TILE + extra, feats), kind) for kind, extra in kinds],
            [VMEM] * (len(sides) + 6),
            [VMEM] * len(sides),
            [row_near, row_near, pltpu.VMEM((len(sides), 8, 3 * TILE), f32)],
        )(*kvs, qg, qg_b, qg_a, stat, st_a, st_b)

    term_b, term_a = terms((2, 1), ((bf16, 16), (bf16, 0)), kv_fb, kv_fa)
    got_b, got_a = pair_swap(term_b, "frame", 1), pair_swap(term_a, "frame", 0)
    (own,) = terms((0,), ((f32, 0),), after(own_kv, term_b))
    sent_q = call(
        query_grad_kernel,
        jax.ShapeDtypeStruct((heads, 2, span, feats), bf16),
        [VMEM] * 6,
        VMEM,
    )(after(qg, got_a), key_near, value_near, attended, column, bias)
    sent = call(
        fold_kernel,
        [jax.ShapeDtypeStruct((4, span, feats), bf16)] * heads,
        [VMEM] * 4,
        [VMEM] * heads,
    )(own, got_b, got_a, sent_q)
    got = [head_swap(sent[k], k) for k in far_first(heads)]

    out = jax.ShapeDtypeStruct((frames_dev * rows_dev, columns // heads, heads * feats), bf16)
    outs = call(assemble_kernel, [out] * 4, [VMEM] * heads, [VMEM] * 4)(*got)
    return tuple(x.reshape((frames_dev, rows_dev) + out.shape[1:]) for x in outs)


def solution(mesh):
    inputs = P("frame", "row", None, "head")
    outputs = P("frame", "row", "head", None)
    return jax.shard_map(
        body,
        mesh=mesh,
        in_specs=(inputs,) * 4 + (P("frame", "row", None, None),),
        out_specs=(outputs,) * 4,
        check_vma=False,
    )
```

```python
import jax
import jax.numpy as jnp
from jax import lax
from jax.experimental import pallas as pl
from jax.experimental.pallas import tpu as pltpu
from jax.sharding import PartitionSpec as P

HEAD_DIM = 128
TILE = 192
SLOTS = 9
WIDE = SLOTS * TILE
SCALE = HEAD_DIM**-0.5
SCALE2 = SCALE * 1.4426950408889634
FAR = 1e30
VMEM_LIMIT = 48 * 1024 * 1024

VMEM = pl.BlockSpec(memory_space=pltpu.VMEM)
SMEM = pl.BlockSpec(memory_space=pltpu.SMEM)


def call(kernel, outs, in_specs, out_specs, scratch=()):
    return pl.pallas_call(
        kernel,
        out_shape=outs,
        in_specs=in_specs,
        out_specs=out_specs,
        scratch_shapes=list(scratch),
        compiler_params=pltpu.CompilerParams(vmem_limit_bytes=VMEM_LIMIT),
    )


def pair_swap(value, axis, parity):
    count = lax.axis_size(axis)
    pairs = []
    for low in range(parity, count - 1, 2):
        pairs += [(low, low + 1), (low + 1, low)]
    return lax.ppermute(value, axis, pairs)


def slot_steps(axis):
    near = 1 - 2 * (lax.axis_index(axis) % 2)
    return (0, near, -near)


def slot_offsets():
    return [(a, b) for a in slot_steps("frame") for b in slot_steps("row")]


def regroup_kernel(a_ref, b_ref, rows_ref, far_ref):
    for ref in (rows_ref, far_ref):
        ref[0 : 2 * TILE, :] = a_ref[...]
        ref[2 * TILE : 4 * TILE, :] = b_ref[...]
    far_ref[4 * TILE :, :] = jnp.zeros((16, far_ref.shape[1]), far_ref.dtype)


def gather_near(tiles, first_ref, second_ref):
    for slot, (ref, start) in enumerate(tiles):
        rows = slice(slot * TILE, (slot + 1) * TILE)
        first_ref[rows, :] = ref[start : start + TILE, :]
        second_ref[rows, :] = ref[start + TILE : start + 2 * TILE, :]


def column_blocks(firsts, seconds, heads):
    group, span = 8 // heads, TILE // heads
    me = lax.axis_index("head")
    row = lax.broadcasted_iota(jnp.int32, (TILE, TILE), 0)
    col = lax.broadcasted_iota(jnp.int32, (TILE, TILE), 1)
    block = jnp.zeros_like(row)
    for d in range(1, heads):
        block += (row >= d * span).astype(jnp.int32)
    inner = row - block * span
    shift = group.bit_length() - 1
    source = (inner >> shift) * 8 + (block ^ me) * group + (inner & (group - 1))
    order = (col == source).astype(jnp.bfloat16)
    joined = jnp.concatenate(firsts + seconds, axis=1)
    moved = jnp.dot(order, joined, preferred_element_type=jnp.float32).astype(jnp.bfloat16)
    feats = joined.shape[1] // 2
    return [
        [moved[k * span : (k + 1) * span, i * feats : (i + 1) * feats] for i in range(2)]
        for k in range(heads)
    ]


def send_order(heads):
    return list(reversed(range(heads)))


def assemble_kernel(*refs):
    heads = len(refs) - 4
    got_refs, out_refs = refs[:heads], refs[heads:]
    feats = got_refs[0].shape[2]
    me = lax.axis_index("head")
    for k, ref in zip(send_order(heads), got_refs):
        place = pl.ds(pl.multiple_of((me ^ k) * feats, HEAD_DIM), feats)
        for i, out_ref in enumerate(out_refs):
            out_ref[:, :, place] = ref[i].reshape(out_ref.shape[:2] + (feats,))


def query_kernel(pairs_s, pairs_v, own_qg, kv, kv_rows, corner_fa, corner_fb, kv_fb, kv_fa, *refs):
    attended_ref, stat_ref, column_ref, bias_ref, key_ref, value_ref = refs
    frame, row = lax.axis_index("frame"), lax.axis_index("row")
    frames, rows = lax.axis_size("frame"), lax.axis_size("row")
    tiles = []
    for own, corners in ((kv, kv_rows), (kv_fa, corner_fa), (kv_fb, corner_fb)):
        tiles += [(own, 0), (corners, 0), (corners, 2 * TILE)]
    gather_near(tiles, key_ref, value_ref)
    lane = lax.broadcasted_iota(jnp.int32, (1, WIDE), 1)
    bias = jnp.zeros((1, WIDE), jnp.float32)
    for slot, (a, b) in enumerate(slot_offsets()):
        bit = pairs_s[0, 0, 0, 9 * (a + 1) + 3 * (b + 1) + 1]
        inside = (frame + a >= 0) & (frame + a < frames) & (row + b >= 0) & (row + b < rows)
        level = jnp.where((bit == 1) & inside, 0.0, -FAR).astype(jnp.float32)
        here = (lane >= slot * TILE) & (lane < (slot + 1) * TILE)
        bias = jnp.where(here, level, bias)
    stat_lane = lax.broadcasted_iota(jnp.int32, (TILE, 128), 1)
    stats = jnp.zeros((TILE, 128), jnp.float32)
    count = own_qg.shape[1] // HEAD_DIM
    for h in range(count):
        feat = slice(h * HEAD_DIM, (h + 1) * HEAD_DIM)
        query, grad = own_qg[0:TILE, feat], own_qg[TILE : 2 * TILE, feat]
        scores = lax.dot_general(
            query, key_ref[:, feat], (((1,), (1,)), ((), ())), preferred_element_type=jnp.float32
        )
        scores = scores * SCALE2 + bias
        top = jnp.max(scores, axis=1, keepdims=True)
        weights = jnp.exp2(scores - top)
        total = jnp.sum(weights, axis=1, keepdims=True)
        rounded = (weights * (1.0 / total)).astype(jnp.bfloat16)
        attended = jnp.dot(rounded, value_ref[:, feat], preferred_element_type=jnp.float32)
        attended = attended.astype(jnp.bfloat16)
        spread = jnp.sum(
            grad.astype(jnp.float32) * attended.astype(jnp.float32), axis=1, keepdims=True
        )
        attended_ref[:, feat] = attended
        stats = jnp.where(stat_lane == h, top + jnp.log2(total), stats)
        stats = jnp.where(stat_lane == count + h, spread, stats)
    bias_ref[...] = bias
    column_ref[...] = stats
    stat_ref[...] = stats.T[0:8, :]
    stat_ref[7:8, 0:27] = pairs_v[0, 0].astype(jnp.float32)


def query_grad_kernel(own_qg, key_ref, value_ref, attended_ref, column_ref, bias_ref, send_ref):
    bias = bias_ref[...]
    count = own_qg.shape[1] // HEAD_DIM
    grad_parts = []
    for h in range(count):
        feat = slice(h * HEAD_DIM, (h + 1) * HEAD_DIM)
        query, grad = own_qg[0:TILE, feat], own_qg[TILE : 2 * TILE, feat]
        key = key_ref[:, feat]
        scores = lax.dot_general(
            query, key, (((1,), (1,)), ((), ())), preferred_element_type=jnp.float32
        )
        weights = jnp.exp2(scores * SCALE2 + bias - column_ref[:, h : h + 1])
        pushes = lax.dot_general(
            grad, value_ref[:, feat], (((1,), (1,)), ((), ())), preferred_element_type=jnp.float32
        )
        spread = column_ref[:, count + h : count + h + 1]
        slopes = (weights * (pushes - spread)).astype(jnp.bfloat16)
        query_grad = SCALE * jnp.dot(slopes, key, preferred_element_type=jnp.float32)
        grad_parts.append(query_grad.astype(jnp.bfloat16))
    blocks = column_blocks([attended_ref[...]], grad_parts, send_ref.shape[0])
    for k, pair in enumerate(blocks):
        for i in range(2):
            send_ref[k, i] = pair[i]


def key_kernel(sides, *refs):
    kvs, refs = refs[: len(sides)], refs[len(sides) :]
    (qg, qg_b, qg_a, st, st_a, st_b), refs = refs[:6], refs[6:]
    outs, (query_ref, grad_ref, stat_ref) = refs[: len(sides)], refs[len(sides) :]
    count = qg.shape[1] // HEAD_DIM
    frame, frames = lax.axis_index("frame"), lax.axis_size("frame")
    gather_near([(qg, 0), (qg_a, 0), (qg_b, 0)], query_ref, grad_ref)
    lane = lax.broadcasted_iota(jnp.int32, (1, TILE), 1)
    level = lax.broadcasted_iota(jnp.int32, (8, TILE), 0)
    frame_steps = [slot_steps("frame")[side] for side in sides]
    for slot, (ref, b) in enumerate(zip((st, st_a, st_b), slot_steps("row"))):
        block = ref[...]
        for i, a in enumerate(frame_steps):
            index = 9 * (a + 1) + 3 * (1 - b) + 1
            bit = jnp.sum(jnp.where(lane == index, block[7:8, :], 0.0), axis=1, keepdims=True)
            inside = (frame + a >= 0) & (frame + a < frames)
            bit = bit * jnp.where(inside, 1.0, 0.0).astype(jnp.float32)
            closed = (level < count) & (bit < 0.5)
            stat_ref[i, :, slot * TILE : (slot + 1) * TILE] = jnp.where(closed, FAR, block)
    for h in range(count):
        feat = slice(h * HEAD_DIM, (h + 1) * HEAD_DIM)
        query, grad = query_ref[:, feat], grad_ref[:, feat]
        keys = jnp.concatenate([ref[0:TILE, feat] for ref in kvs], axis=0)
        values = jnp.concatenate([ref[TILE : 2 * TILE, feat] for ref in kvs], axis=0)
        scores = lax.dot_general(
            keys, query, (((1,), (1,)), ((), ())), preferred_element_type=jnp.float32
        )
        pushes = lax.dot_general(
            values, grad, (((1,), (1,)), ((), ())), preferred_element_type=jnp.float32
        )
        rounded, slopes = [], []
        for i in range(len(sides)):
            rows = slice(i * TILE, (i + 1) * TILE)
            weights = jnp.exp2(scores[rows] * SCALE2 - stat_ref[i, h : h + 1, :])
            spread = stat_ref[i, count + h : count + h + 1, :]
            rounded.append(weights.astype(jnp.bfloat16))
            slopes.append((weights * (pushes[rows] - spread)).astype(jnp.bfloat16))
        rounded, slopes = jnp.concatenate(rounded, axis=0), jnp.concatenate(slopes, axis=0)
        value_grad = jnp.dot(rounded, grad, preferred_element_type=jnp.float32)
        key_grad = SCALE * jnp.dot(slopes, query, preferred_element_type=jnp.float32)
        for i, ref in enumerate(outs):
            rows = slice(i * TILE, (i + 1) * TILE)
            if ref.shape[0] > 2 * TILE:
                ref[2 * TILE :, feat] = jnp.zeros((16, HEAD_DIM), ref.dtype)
            ref[0:TILE, feat] = key_grad[rows].astype(ref.dtype)
            ref[TILE : 2 * TILE, feat] = value_grad[rows].astype(ref.dtype)


def fold_kernel(own_ref, got_b, got_a, query_blocks, *send_refs):
    total = own_ref[...] + got_a[...].astype(jnp.float32)
    total += got_b[0 : 2 * TILE, :].astype(jnp.float32)
    total = total.astype(jnp.bfloat16)
    blocks = column_blocks([total[0:TILE]], [total[TILE : 2 * TILE]], len(send_refs))
    for k, ref in enumerate(send_refs):
        for i in range(2):
            ref[i] = query_blocks[k, i]
            ref[2 + i] = blocks[k][i]


def after(value, *others):
    return lax.optimization_barrier((value,) + others)[0]


def head_swap(value, k):
    count = lax.axis_size("head")
    return lax.ppermute(value, "head", [(i, i ^ k) for i in range(count)]) if k else value


def stacked(first, second):
    rows = first.shape[0]
    low = jnp.pad(first, ((0, rows), (0, 0)), constant_values=-jnp.inf)
    return jnp.maximum(low, jnp.pad(second, ((rows, 0), (0, 0)), constant_values=-jnp.inf))


def body(queries, key_tokens, value_tokens, grad_out, tile_pairs):
    frames_dev, rows_dev, columns, feats = queries.shape
    heads = lax.axis_size("head")
    bf16, f32 = jnp.bfloat16, jnp.float32
    flat = [x.reshape(TILE, feats) for x in (key_tokens, value_tokens, queries, grad_out)]

    own_kv = stacked(flat[0], flat[1])
    kv_a, kv_b = pair_swap(own_kv, "row", 0), pair_swap(own_kv, "row", 1)
    kv_fb, kv_fa = pair_swap(own_kv, "frame", 1), pair_swap(own_kv, "frame", 0)
    qg = stacked(flat[2], flat[3])
    two = [jax.ShapeDtypeStruct((4 * TILE + extra, feats), bf16) for extra in (0, 16)]
    rows, far_rows = call(regroup_kernel, two, [VMEM] * 2, (VMEM, VMEM))(after(kv_a, qg), kv_b)
    corner_fb = pair_swap(far_rows, "frame", 1)
    corner_fa = pair_swap(after(rows, kv_fb, kv_fa), "frame", 0)
    qg_late = after(qg, rows)
    qg_b, qg_a = pair_swap(qg_late, "row", 1), pair_swap(qg_late, "row", 0)

    span = TILE // heads
    wide = jax.ShapeDtypeStruct((WIDE, feats), bf16)
    attended, stat, column, bias, key_near, value_near = call(
        query_kernel,
        (
            jax.ShapeDtypeStruct((TILE, feats), bf16),
            jax.ShapeDtypeStruct((8, TILE), f32),
            jax.ShapeDtypeStruct((TILE, 128), f32),
            jax.ShapeDtypeStruct((1, WIDE), f32),
            wide,
            wide,
        ),
        [SMEM] + [VMEM] * 8,
        (VMEM,) * 6,
    )(tile_pairs, tile_pairs, qg, own_kv, rows, corner_fa, corner_fb, kv_fb, kv_fa)
    st_a, st_b = pair_swap(stat, "row", 0), pair_swap(stat, "row", 1)

    def terms(sides, kinds, *kvs):
        row_near = pltpu.VMEM((3 * TILE, feats), bf16)
        return call(
            lambda *refs: key_kernel(sides, *refs),
            [jax.ShapeDtypeStruct((2 * TILE + extra, feats), kind) for kind, extra in kinds],
            [VMEM] * (len(sides) + 6),
            [VMEM] * len(sides),
            [row_near, row_near, pltpu.VMEM((len(sides), 8, 3 * TILE), f32)],
        )(*kvs, qg, qg_b, qg_a, stat, st_a, st_b)

    term_b, term_a = terms((2, 1), ((bf16, 16), (bf16, 0)), kv_fb, kv_fa)
    got_b, got_a = pair_swap(term_b, "frame", 1), pair_swap(term_a, "frame", 0)
    (own,) = terms((0,), ((f32, 0),), after(own_kv, term_b))
    sent_q = call(
        query_grad_kernel,
        jax.ShapeDtypeStruct((heads, 2, span, feats), bf16),
        [VMEM] * 6,
        VMEM,
    )(after(qg, got_a), key_near, value_near, attended, column, bias)
    sent = call(
        fold_kernel,
        [jax.ShapeDtypeStruct((4, span, feats), bf16)] * heads,
        [VMEM] * 4,
        [VMEM] * heads,
    )(own, got_b, got_a, sent_q)
    got = [head_swap(sent[k], k) for k in send_order(heads)]

    out = jax.ShapeDtypeStruct((frames_dev * rows_dev, columns // heads, heads * feats), bf16)
    outs = call(assemble_kernel, [out] * 4, [VMEM] * heads, [VMEM] * 4)(*got)
    return tuple(x.reshape((frames_dev, rows_dev) + out.shape[1:]) for x in outs)


def solution(mesh):
    inputs = P("frame", "row", None, "head")
    outputs = P("frame", "row", "head", None)
    return jax.shard_map(
        body,
        mesh=mesh,
        in_specs=(inputs,) * 4 + (P("frame", "row", None, None),),
        out_specs=(outputs,) * 4,
        check_vma=False,
    )
```

```python
import jax
import jax.numpy as jnp
from jax import lax
from jax.experimental import pallas as pl
from jax.experimental.pallas import tpu as pltpu
from jax.sharding import PartitionSpec as P

HEAD_DIM = 128
TILE = 192
SLOTS = 9
WIDE = SLOTS * TILE
SCALE = HEAD_DIM**-0.5
SCALE2 = SCALE * 1.4426950408889634
FAR = 1e30
VMEM_LIMIT = 48 * 1024 * 1024

VMEM = pl.BlockSpec(memory_space=pltpu.VMEM)
SMEM = pl.BlockSpec(memory_space=pltpu.SMEM)


def call(kernel, outs, in_specs, out_specs, scratch=()):
    return pl.pallas_call(
        kernel,
        out_shape=outs,
        in_specs=in_specs,
        out_specs=out_specs,
        scratch_shapes=list(scratch),
        compiler_params=pltpu.CompilerParams(vmem_limit_bytes=VMEM_LIMIT),
    )


def pair_swap(value, axis, parity):
    count = lax.axis_size(axis)
    pairs = []
    for low in range(parity, count - 1, 2):
        pairs += [(low, low + 1), (low + 1, low)]
    return lax.ppermute(value, axis, pairs)


def slot_steps(axis):
    near = 1 - 2 * (lax.axis_index(axis) % 2)
    return (0, near, -near)


def slot_offsets():
    return [(a, b) for a in slot_steps("frame") for b in slot_steps("row")]


def regroup_kernel(a_ref, b_ref, rows_ref, far_ref):
    for ref in (rows_ref, far_ref):
        ref[0 : 2 * TILE, :] = a_ref[...]
        ref[2 * TILE : 4 * TILE, :] = b_ref[...]
    far_ref[4 * TILE :, :] = jnp.zeros((16, far_ref.shape[1]), far_ref.dtype)


def gather_near(tiles, first_ref, second_ref):
    for slot, (ref, start) in enumerate(tiles):
        rows = slice(slot * TILE, (slot + 1) * TILE)
        first_ref[rows, :] = ref[start : start + TILE, :]
        second_ref[rows, :] = ref[start + TILE : start + 2 * TILE, :]


def column_blocks(firsts, seconds, heads):
    group, span = 8 // heads, TILE // heads
    me = lax.axis_index("head")
    row = lax.broadcasted_iota(jnp.int32, (TILE, TILE), 0)
    col = lax.broadcasted_iota(jnp.int32, (TILE, TILE), 1)
    block = jnp.zeros_like(row)
    for d in range(1, heads):
        block += (row >= d * span).astype(jnp.int32)
    inner = row - block * span
    shift = group.bit_length() - 1
    source = (inner >> shift) * 8 + (block ^ me) * group + (inner & (group - 1))
    order = (col == source).astype(jnp.bfloat16)
    joined = jnp.concatenate(firsts + seconds, axis=1)
    moved = jnp.dot(order, joined, preferred_element_type=jnp.float32).astype(jnp.bfloat16)
    feats = joined.shape[1] // 2
    return [
        [moved[k * span : (k + 1) * span, i * feats : (i + 1) * feats] for i in range(2)]
        for k in range(heads)
    ]


def far_first(heads):
    return [heads // 2] + [k for k in reversed(range(heads)) if k != heads // 2]


def assemble_kernel(*refs):
    heads = len(refs) - 4
    got_refs, out_refs = refs[:heads], refs[heads:]
    feats = got_refs[0].shape[2]
    me = lax.axis_index("head")
    for k, ref in zip(far_first(heads), got_refs):
        place = pl.ds(pl.multiple_of((me ^ k) * feats, HEAD_DIM), feats)
        for i, out_ref in enumerate(out_refs):
            out_ref[:, :, place] = ref[i].reshape(out_ref.shape[:2] + (feats,))


def query_kernel(pairs_s, pairs_v, own_qg, kv, kv_rows, corner_fa, corner_fb, kv_fb, kv_fa, *refs):
    attended_ref, stat_ref, column_ref, bias_ref, key_ref, value_ref = refs
    frame, row = lax.axis_index("frame"), lax.axis_index("row")
    frames, rows = lax.axis_size("frame"), lax.axis_size("row")
    tiles = []
    for own, corners in ((kv, kv_rows), (kv_fa, corner_fa), (kv_fb, corner_fb)):
        tiles += [(own, 0), (corners, 0), (corners, 2 * TILE)]
    gather_near(tiles, key_ref, value_ref)
    lane = lax.broadcasted_iota(jnp.int32, (1, WIDE), 1)
    bias = jnp.zeros((1, WIDE), jnp.float32)
    for slot, (a, b) in enumerate(slot_offsets()):
        bit = pairs_s[0, 0, 0, 9 * (a + 1) + 3 * (b + 1) + 1]
        inside = (frame + a >= 0) & (frame + a < frames) & (row + b >= 0) & (row + b < rows)
        level = jnp.where((bit == 1) & inside, 0.0, -FAR).astype(jnp.float32)
        here = (lane >= slot * TILE) & (lane < (slot + 1) * TILE)
        bias = jnp.where(here, level, bias)
    stat_lane = lax.broadcasted_iota(jnp.int32, (TILE, 128), 1)
    stats = jnp.zeros((TILE, 128), jnp.float32)
    count = own_qg.shape[1] // HEAD_DIM
    for h in range(count):
        feat = slice(h * HEAD_DIM, (h + 1) * HEAD_DIM)
        query, grad = own_qg[0:TILE, feat], own_qg[TILE : 2 * TILE, feat]
        scores = lax.dot_general(
            query, key_ref[:, feat], (((1,), (1,)), ((), ())), preferred_element_type=jnp.float32
        )
        scores = scores * SCALE2 + bias
        top = jnp.max(scores, axis=1, keepdims=True)
        weights = jnp.exp2(scores - top)
        total = jnp.sum(weights, axis=1, keepdims=True)
        rounded = (weights * (1.0 / total)).astype(jnp.bfloat16)
        attended = jnp.dot(rounded, value_ref[:, feat], preferred_element_type=jnp.float32)
        attended = attended.astype(jnp.bfloat16)
        spread = jnp.sum(
            grad.astype(jnp.float32) * attended.astype(jnp.float32), axis=1, keepdims=True
        )
        attended_ref[:, feat] = attended
        stats = jnp.where(stat_lane == h, top + jnp.log2(total), stats)
        stats = jnp.where(stat_lane == count + h, spread, stats)
    bias_ref[...] = bias
    column_ref[...] = stats
    stat_ref[...] = stats.T[0:8, :]
    stat_ref[7:8, 0:27] = pairs_v[0, 0].astype(jnp.float32)


def query_grad_kernel(own_qg, key_ref, value_ref, attended_ref, column_ref, bias_ref, send_ref):
    bias = bias_ref[...]
    count = own_qg.shape[1] // HEAD_DIM
    grad_parts = []
    for h in range(count):
        feat = slice(h * HEAD_DIM, (h + 1) * HEAD_DIM)
        query, grad = own_qg[0:TILE, feat], own_qg[TILE : 2 * TILE, feat]
        key = key_ref[:, feat]
        scores = lax.dot_general(
            query, key, (((1,), (1,)), ((), ())), preferred_element_type=jnp.float32
        )
        weights = jnp.exp2(scores * SCALE2 + bias - column_ref[:, h : h + 1])
        pushes = lax.dot_general(
            grad, value_ref[:, feat], (((1,), (1,)), ((), ())), preferred_element_type=jnp.float32
        )
        spread = column_ref[:, count + h : count + h + 1]
        slopes = (weights * (pushes - spread)).astype(jnp.bfloat16)
        query_grad = SCALE * jnp.dot(slopes, key, preferred_element_type=jnp.float32)
        grad_parts.append(query_grad.astype(jnp.bfloat16))
    blocks = column_blocks([attended_ref[...]], grad_parts, send_ref.shape[0])
    for k, pair in enumerate(blocks):
        for i in range(2):
            send_ref[k, i] = pair[i]


def key_kernel(sides, *refs):
    kvs, refs = refs[: len(sides)], refs[len(sides) :]
    (qg, qg_b, qg_a, st, st_a, st_b), refs = refs[:6], refs[6:]
    outs, (query_ref, grad_ref, stat_ref) = refs[: len(sides)], refs[len(sides) :]
    count = qg.shape[1] // HEAD_DIM
    frame, frames = lax.axis_index("frame"), lax.axis_size("frame")
    gather_near([(qg, 0), (qg_a, 0), (qg_b, 0)], query_ref, grad_ref)
    lane = lax.broadcasted_iota(jnp.int32, (1, TILE), 1)
    level = lax.broadcasted_iota(jnp.int32, (8, TILE), 0)
    frame_steps = [slot_steps("frame")[side] for side in sides]
    for slot, (ref, b) in enumerate(zip((st, st_a, st_b), slot_steps("row"))):
        block = ref[...]
        for i, a in enumerate(frame_steps):
            index = 9 * (a + 1) + 3 * (1 - b) + 1
            bit = jnp.sum(jnp.where(lane == index, block[7:8, :], 0.0), axis=1, keepdims=True)
            inside = (frame + a >= 0) & (frame + a < frames)
            bit = bit * jnp.where(inside, 1.0, 0.0).astype(jnp.float32)
            closed = (level < count) & (bit < 0.5)
            stat_ref[i, :, slot * TILE : (slot + 1) * TILE] = jnp.where(closed, FAR, block)
    for h in range(count):
        feat = slice(h * HEAD_DIM, (h + 1) * HEAD_DIM)
        query, grad = query_ref[:, feat], grad_ref[:, feat]
        keys = jnp.concatenate([ref[0:TILE, feat] for ref in kvs], axis=0)
        values = jnp.concatenate([ref[TILE : 2 * TILE, feat] for ref in kvs], axis=0)
        scores = lax.dot_general(
            keys, query, (((1,), (1,)), ((), ())), preferred_element_type=jnp.float32
        )
        pushes = lax.dot_general(
            values, grad, (((1,), (1,)), ((), ())), preferred_element_type=jnp.float32
        )
        rounded, slopes = [], []
        for i in range(len(sides)):
            rows = slice(i * TILE, (i + 1) * TILE)
            weights = jnp.exp2(scores[rows] * SCALE2 - stat_ref[i, h : h + 1, :])
            spread = stat_ref[i, count + h : count + h + 1, :]
            rounded.append(weights.astype(jnp.bfloat16))
            slopes.append((weights * (pushes[rows] - spread)).astype(jnp.bfloat16))
        rounded, slopes = jnp.concatenate(rounded, axis=0), jnp.concatenate(slopes, axis=0)
        value_grad = jnp.dot(rounded, grad, preferred_element_type=jnp.float32)
        key_grad = SCALE * jnp.dot(slopes, query, preferred_element_type=jnp.float32)
        for i, ref in enumerate(outs):
            rows = slice(i * TILE, (i + 1) * TILE)
            if ref.shape[0] > 2 * TILE:
                ref[2 * TILE :, feat] = jnp.zeros((16, HEAD_DIM), ref.dtype)
            ref[0:TILE, feat] = key_grad[rows].astype(ref.dtype)
            ref[TILE : 2 * TILE, feat] = value_grad[rows].astype(ref.dtype)


def fold_kernel(own_ref, got_b, got_a, query_blocks, *send_refs):
    total = own_ref[...] + got_a[...].astype(jnp.float32)
    total += got_b[0 : 2 * TILE, :].astype(jnp.float32)
    total = total.astype(jnp.bfloat16)
    blocks = column_blocks([total[0:TILE]], [total[TILE : 2 * TILE]], len(send_refs))
    for k, ref in enumerate(send_refs):
        for i in range(2):
            ref[i] = query_blocks[k, i]
            ref[2 + i] = blocks[k][i]


def after(value, *others):
    return lax.optimization_barrier((value,) + others)[0]


def head_swap(value, k):
    count = lax.axis_size("head")
    return lax.ppermute(value, "head", [(i, i ^ k) for i in range(count)]) if k else value


def stacked(first, second):
    rows = first.shape[0]
    low = jnp.pad(first, ((0, rows), (0, 0)), constant_values=-jnp.inf)
    return jnp.maximum(low, jnp.pad(second, ((rows, 0), (0, 0)), constant_values=-jnp.inf))


def body(queries, key_tokens, value_tokens, grad_out, tile_pairs):
    frames_dev, rows_dev, columns, feats = queries.shape
    heads = lax.axis_size("head")
    bf16, f32 = jnp.bfloat16, jnp.float32
    flat = [x.reshape(TILE, feats) for x in (key_tokens, value_tokens, queries, grad_out)]

    own_kv = stacked(flat[0], flat[1])
    kv_a, kv_b = pair_swap(own_kv, "row", 0), pair_swap(own_kv, "row", 1)
    kv_fb, kv_fa = pair_swap(own_kv, "frame", 1), pair_swap(own_kv, "frame", 0)
    qg = stacked(flat[2], flat[3])
    two = [jax.ShapeDtypeStruct((4 * TILE + extra, feats), bf16) for extra in (0, 16)]
    rows, far_rows = call(regroup_kernel, two, [VMEM] * 2, (VMEM, VMEM))(after(kv_a, qg), kv_b)
    corner_fb = pair_swap(far_rows, "frame", 1)
    corner_fa = pair_swap(after(rows, kv_fb, kv_fa), "frame", 0)
    qg_late = after(qg, rows)
    qg_b, qg_a = pair_swap(qg_late, "row", 1), pair_swap(qg_late, "row", 0)

    span = TILE // heads
    wide = jax.ShapeDtypeStruct((WIDE, feats), bf16)
    attended, stat, column, bias, key_near, value_near = call(
        query_kernel,
        (
            jax.ShapeDtypeStruct((TILE, feats), bf16),
            jax.ShapeDtypeStruct((8, TILE), f32),
            jax.ShapeDtypeStruct((TILE, 128), f32),
            jax.ShapeDtypeStruct((1, WIDE), f32),
            wide,
            wide,
        ),
        [SMEM] + [VMEM] * 8,
        (VMEM,) * 6,
    )(tile_pairs, tile_pairs, qg, own_kv, rows, corner_fa, corner_fb, kv_fb, kv_fa)
    st_a, st_b = pair_swap(stat, "row", 0), pair_swap(stat, "row", 1)

    def terms(sides, kinds, *kvs):
        row_near = pltpu.VMEM((3 * TILE, feats), bf16)
        return call(
            lambda *refs: key_kernel(sides, *refs),
            [jax.ShapeDtypeStruct((2 * TILE + extra, feats), kind) for kind, extra in kinds],
            [VMEM] * (len(sides) + 6),
            [VMEM] * len(sides),
            [row_near, row_near, pltpu.VMEM((len(sides), 8, 3 * TILE), f32)],
        )(*kvs, qg, qg_b, qg_a, stat, st_a, st_b)

    term_b, term_a = terms((2, 1), ((bf16, 16), (bf16, 0)), kv_fb, kv_fa)
    got_b, got_a = pair_swap(term_b, "frame", 1), pair_swap(term_a, "frame", 0)
    (own,) = terms((0,), ((f32, 0),), after(own_kv, term_b))
    sent_q = call(
        query_grad_kernel,
        jax.ShapeDtypeStruct((heads, 2, span, feats), bf16),
        [VMEM] * 6,
        VMEM,
    )(after(qg, term_b), key_near, value_near, attended, column, bias)
    sent = call(
        fold_kernel,
        [jax.ShapeDtypeStruct((4, span, feats), bf16)] * heads,
        [VMEM] * 4,
        [VMEM] * heads,
    )(own, got_b, got_a, sent_q)
    got = [head_swap(sent[k], k) for k in far_first(heads)]

    out = jax.ShapeDtypeStruct((frames_dev * rows_dev, columns // heads, heads * feats), bf16)
    outs = call(assemble_kernel, [out] * 4, [VMEM] * heads, [VMEM] * 4)(*got)
    return tuple(x.reshape((frames_dev, rows_dev) + out.shape[1:]) for x in outs)


def solution(mesh):
    inputs = P("frame", "row", None, "head")
    outputs = P("frame", "row", "head", None)
    return jax.shard_map(
        body,
        mesh=mesh,
        in_specs=(inputs,) * 4 + (P("frame", "row", None, None),),
        out_specs=(outputs,) * 4,
        check_vma=False,
    )
```
